256 devices in a mesh: side: 2 (over core), head: 64 (over z, x_lo, y), sub: 2 (over x_hi).
Axes of the slice: x: 4 (x_hi: 2, x_lo: 2; x = x_hi * 2 + x_lo), y: 4, z: 8, core: 2. Of those that a mesh axis runs over, the one named last changes fastest.
Arguments:
- queries: bfloat16 [2, 512, 64, 576], P('sub', None, 'head'), may hold values from -1500 to 1500
- cache_pool: bfloat16 [2, 1024, 64, 576], P('sub', 'head'), may hold values from -7 to 7
- block_table: int32 [2, 512, 2], P('sub', 'head'), may hold values from 0 to 15, as said below
- cache_len: int32 [2, 512], P('sub', 'head'), may hold values from 1 to 128, 32768 in all within a row
- w_uv: bfloat16 [64, 512, 128], P('head'), may hold values from -0.75 to 0.75
- w_out: bfloat16 [64, 128, 7168], P('head'), may hold values from -0.125 to 0.125
- residual: bfloat16 [2, 512, 7168], P('sub', 'head'), may hold values from -6 to 6
- norm_gain: float32 [7168], replicated, may hold values from 0.1 to 1.9
- expert_ids: int32 [2, 512, 4], P('sub', 'head'), may hold values from 0 to 7, all different within a row; in each aligned block of 8 rows (0 to 7, 8 to 15, ..., all dimensions but the last counted through in order) at most 8 rows name the same one
- expert_gates: float32 [2, 512, 4], P('sub', 'head'), may hold values from 0.1 to 1
- w_gate: bfloat16 [64, 7168, 128], P('head'), may hold values from -0.0625 to 0.0625
- w_up: bfloat16 [64, 7168, 128], P('head'), may hold values from -0.0625 to 0.0625
- w_down: bfloat16 [64, 128, 7168], P('head'), may hold values from -0.375 to 0.375
Outputs:
- layer_out: bfloat16 [2, 2, 512, 7168], P('side', 'sub', 'head')
The draws below stay inside these ranges and needn't reach their ends.
Inputs may be any that keep to these rules, and one draw needn't show every extreme that they name: `block_table`: the block table entries of the 8 rows of one owner name each of that owner's 16 blocks exactly once. `cache_len`: the 512 lengths of each half sum to 32768, and the longest is 128. `expert_ids`: each row names 4 different experts; the 8 rows of one device name one expert at most 8 times, and that bound is reached.
All inputs are finite; a program needn't handle non-finite values. No bound on the sum of `cache_len` on one device may be relied on, other than what follows from the above.
Results may differ from the reference program's by a relative error of at most 0.009.
Values may be sent and summed in bfloat16 or wider, within the bound.
A program may use at most 192 MiB of HBM per device.

```python
import math
import jax
import jax.numpy as jnp
import numpy as np
from jax import lax

D = 7168
LAT = 512
VH = 128
KW = 576
HEADS = 64
FFW = 1024
PIECES = 8
UNITS = 128
EXPERTS = 8
TOP = 4
OWN = 8
CAP = 8
BLK = 64
MAXBLK = 2
LMAX = 128
NBLK_DEV = 16
HALVES = 2
HALF_ROWS = 512
POOL = 1024


def table_draw(key):
    key = jax.random.fold_in(key, 21)
    splits = jax.random.split(key, HALVES * (HALF_ROWS // OWN))
    orders = jax.vmap(lambda sub_key: jax.random.permutation(sub_key, NBLK_DEV))(splits)
    return orders.reshape(HALVES, HALF_ROWS, MAXBLK).astype(jnp.int32)


def cache_base(key):
    key = jax.random.fold_in(key, 22)
    return jnp.clip(jax.random.normal(key, (HALVES, POOL, BLK, KW), jnp.float32), -6.0, 6.0)


def draw_block_table(key, part):
    shared = table_draw(key)
    return shared


def draw_cache_pool(key, part):
    base = cache_base(key)
    return base.astype(jnp.bfloat16)


def draw_queries(key, part):
    key = jax.random.fold_in(key, 3)
    query = jnp.clip(jax.random.normal(key, (HALVES, HALF_ROWS, HEADS, KW), jnp.float32), -6.0, 6.0)
    return query.astype(jnp.bfloat16)


def block_levels(rng, shape, pieces, least, largest):
    gain = 1.0
    for dim, parts in pieces:
        steps = jax.random.uniform(jax.random.fold_in(jax.random.fold_in(rng, 6), dim), (parts,), jnp.float32, least / len(pieces), largest / len(pieces))
        gain = gain * jnp.repeat(jnp.exp(steps), shape[dim] // parts).reshape((-1,) + (1,) * (len(shape) - 1 - dim))
    return gain


def split_up(count, total, most, slope):
    weights = [(1 << 20) // math.isqrt(rank ** slope) + 1 for rank in range(2, count + 1)]
    surplus, counts = total - most - (count - 1), [1] * (count - 1)
    while surplus > 0:
        candidates = [i for i in range(count - 1) if counts[i] < most]
        whole, remaining = sum([weights[i] for i in candidates]), surplus
        for i in candidates:
            addition = min(most - counts[i], max(1, remaining * weights[i] // whole), surplus)
            counts[i] = counts[i] + addition
            surplus = surplus - addition
    return np.array([most] + counts)


def ragged(rng, count, total, limit, slope):
    if count == 2:
        one = jax.random.randint(rng, (), max(1, total - limit), min(limit, total - 1) + 1)
        return jnp.stack([one, total - one])
    sizes = jnp.asarray(split_up(count, total, limit, slope), jnp.int32)
    twos = (count - 1) // 2
    giver, sink = sizes[1:1 + 2 * twos:2], sizes[2:2 + 2 * twos:2]
    margin = jnp.minimum(giver - 1, limit - sink)
    moved = jax.random.randint(jax.random.fold_in(rng, 1), (twos,), 0, 1 << 20) % (margin + 1)
    sizes = sizes.at[1:1 + 2 * twos:2].set(giver - moved).at[2:2 + 2 * twos:2].set(sink + moved)
    return sizes[jax.random.permutation(jax.random.fold_in(rng, 2), count)]


def shared_out(rng, own, number, rows, count, top, reach, lean):
    order = jax.random.permutation(rng, count)
    packed, ordinary = shares(count, rows * top, reach, lean, True), shares(count, rows * top, reach, lean, False)
    places = jnp.arange(count)

    def named(sizes, turn):
        used = int((sizes > 0).sum())
        fixed = max(1, used // 4)
        moved = fixed + (places - fixed + turn * (used - fixed)) % max(1, count - fixed)
        return jnp.zeros((count,), jnp.int32).at[order[jnp.where(places < fixed, places, moved)]].set(jnp.asarray(sizes, jnp.int32))

    sizes = jnp.where(number % 4 == 0, named(packed, number // 4), named(ordinary, number - number // 4 - 1))
    mixed = jax.random.permutation(jax.random.fold_in(own, 3), count)
    giver, taker = mixed[0:count // 2 * 2:2], mixed[1:count // 2 * 2:2]
    slack = jnp.minimum(sizes[giver] - 1, reach - sizes[taker]) // 2
    slack = jnp.where((giver == order[0]) | (taker == order[0]) | (sizes[taker] == 0), 0, jnp.maximum(slack, 0))
    moved = jax.random.randint(jax.random.fold_in(own, 4), (count // 2,), 0, 1 << 20) % (slack + 1)
    sizes = sizes.at[giver].add(-moved).at[taker].add(moved)
    members = jnp.searchsorted(jnp.cumsum(sizes), jnp.arange(rows * top), side="right").astype(jnp.int32)
    table = members.reshape(top, rows).T
    table = table[jax.random.permutation(jax.random.fold_in(own, 1), rows)]
    turn = jax.random.randint(jax.random.fold_in(own, 2), (rows, 1), 0, top)
    return jnp.take_along_axis(table, (jnp.arange(top)[None, :] + turn) % top, axis=1)


def shares(amount, total, reach, skew, full):
    loads = [(1 << 20) // math.isqrt(standing ** skew) + 1 for standing in range(1, amount + 1)]
    largest = reach if full else min(reach, max(-(-total // amount), total * loads[0] // sum(loads)))
    least = 1 if total - largest >= amount - 1 else 0
    counts, surplus = [largest] + [least] * (amount - 1), total - largest - least * (amount - 1)
    while surplus > 0:
        free = [i for i in range(1, amount) if counts[i] < largest] or [i for i in range(1, amount) if counts[i] < reach]
        mass, remaining = sum([loads[i] for i in free]), surplus
        for i in free:
            addition = min(reach - counts[i], max(1, remaining * loads[i] // mass), surplus)
            counts[i] = counts[i] + addition
            surplus = surplus - addition
    return np.array(counts)


def centred(own_key, shape, deviation, limit, cuts=(), held_as=jnp.bfloat16):
    drawn = jax.random.normal(own_key, shape, jnp.float32) * deviation
    if len(cuts) > 0:
        drawn = block_levels(own_key, shape, cuts, -0.22, 0.18) * drawn
    return jnp.clip(drawn, min=-limit, max=limit).astype(held_as)


def setup_inputs(seed: int = 0) -> dict:
    seeds = jax.random.split(jax.random.key(seed), 14)
    queries = draw_queries(jax.random.fold_in(seeds[13], 71), 0)
    cache_pool = draw_cache_pool(jax.random.fold_in(seeds[13], 71), 0)
    block_table = draw_block_table(jax.random.fold_in(seeds[13], 71), 0)
    cache_len = jax.vmap(lambda own: ragged(own, HALF_ROWS, HALF_ROWS * LMAX // 2, LMAX, 2))(jax.random.split(seeds[3], HALVES)).reshape((HALVES, HALF_ROWS)).astype(jnp.int32)
    w_uv = centred(seeds[4], (HEADS, LAT, VH), (LAT // 8) ** -0.5, 0.75, ((0, 64),))
    w_out = centred(seeds[5], (HEADS, VH, D), (HEADS * VH // 4) ** -0.5, 0.125, ((0, 64),))
    residual = centred(seeds[6], (HALVES, HALF_ROWS, D), 1.0, 6.0, ((0, 2), (1, 64)))
    norm_gain = jnp.clip(1.0 + 0.18 * jax.random.normal(seeds[7], (D,), jnp.float32), 0.1, 1.9)
    expert_ids_keys = jax.random.split(jax.random.fold_in(seeds[8], 1), HALVES * HALF_ROWS // OWN)
    expert_ids_turns = jax.random.permutation(jax.random.fold_in(seeds[8], 3), HALVES * HALF_ROWS // OWN)
    expert_ids = jax.vmap(lambda own, number: shared_out(jax.random.fold_in(seeds[8], 2), own, number, OWN, EXPERTS, TOP, CAP, 2))(expert_ids_keys, expert_ids_turns).reshape((HALVES, HALF_ROWS, TOP))
    expert_gates = jnp.clip(0.1 + 0.9 * jax.random.uniform(seeds[9], (HALVES, HALF_ROWS, TOP), jnp.float32) ** block_levels(seeds[9], (HALVES, HALF_ROWS, TOP), ((0, 2), (1, 64)), -0.2, 0.2), 0.1, 1.0)
    w_gate = centred(seeds[10], (EXPERTS * PIECES, D, UNITS), D ** -0.5, 0.0625, ((0, 64),))
    w_up = centred(seeds[11], (EXPERTS * PIECES, D, UNITS), D ** -0.5, 0.0625, ((0, 64),))
    w_down = centred(seeds[12], (EXPERTS * PIECES, UNITS, D), (FFW // 4) ** -0.5, 0.375, ((0, 64),))
    return {"queries": queries, "cache_pool": cache_pool, "block_table": block_table, "cache_len": cache_len, "w_uv": w_uv, "w_out": w_out, "residual": residual, "norm_gain": norm_gain, "expert_ids": expert_ids, "expert_gates": expert_gates, "w_gate": w_gate, "w_up": w_up, "w_down": w_down}


score_scale = 192 ** (-0.5)

def reference(queries, cache_pool, block_table, cache_len, w_uv, w_out, residual, norm_gain, expert_ids, expert_gates, w_gate, w_up, w_down):
    highest = lax.Precision.HIGHEST
    row_index = jnp.arange(HALF_ROWS, dtype=jnp.int32)
    owner_base = row_index // OWN * NBLK_DEV
    global_blocks = (owner_base[None, :, None] + block_table).astype(jnp.int32)
    positions = jnp.arange(LMAX, dtype=jnp.int32)

    def one_half(operands):
        pool_half, blocks, query, lengths = operands
        key_rows = pool_half[blocks].reshape(HALF_ROWS, LMAX, KW)
        scores = jnp.einsum('rhk,rpk->rhp', query.astype(jnp.float32), key_rows.astype(jnp.float32), precision=highest) * score_scale
        visible = positions[None, :] < lengths[:, None]
        scores = jnp.where(visible[:, None, :], scores, -1e+30)
        peak = lax.optimization_barrier(jnp.max(scores, axis=-1, keepdims=True))
        raw_weights = jnp.exp(scores - peak) * visible[:, None, :].astype(jnp.float32)
        weights = raw_weights / lax.optimization_barrier(jnp.sum(raw_weights, axis=-1, keepdims=True))
        latent = jnp.einsum('rhp,rpc->rhc', weights, key_rows[:, :, :LAT].astype(jnp.float32), precision=highest)
        return latent.astype(jnp.bfloat16)
    latents = lax.map(one_half, (cache_pool, global_blocks, queries, cache_len))
    head_out = jnp.einsum('srhc,hcv->srhv', latents.astype(jnp.float32), w_uv.astype(jnp.float32), precision=highest).astype(jnp.bfloat16)
    attended = jnp.einsum('srhv,hvd->srd', head_out.astype(jnp.float32), w_out.astype(jnp.float32), precision=highest)
    stream = (residual.astype(jnp.float32) + attended).astype(jnp.bfloat16)
    stream_f = stream.astype(jnp.float32)
    mean_square = lax.optimization_barrier(jnp.mean(stream_f * stream_f, axis=-1, keepdims=True))
    normed = (stream_f * lax.rsqrt(mean_square + 1e-06) * norm_gain).astype(jnp.bfloat16)
    flat_rows = normed.reshape(-1, D).astype(jnp.float32)
    picked = (expert_ids[..., None] == jnp.arange(EXPERTS, dtype=jnp.int32)).astype(jnp.float32)
    selection = lax.optimization_barrier(jnp.sum(expert_gates[..., None] * picked, axis=2)).reshape(-1, EXPERTS)
    mixture = jnp.zeros((flat_rows.shape[0], D), jnp.float32)
    for expert in range(EXPERTS):
        lower = expert * PIECES
        gate_part = jnp.einsum('td,pdu->tpu', flat_rows, w_gate[lower:lower + PIECES].astype(jnp.float32), precision=highest)
        up_part = jnp.einsum('td,pdu->tpu', flat_rows, w_up[lower:lower + PIECES].astype(jnp.float32), precision=highest)
        hidden = (jax.nn.silu(gate_part) * up_part).astype(jnp.bfloat16)
        piece_out = jnp.einsum('tpu,pud->tpd', hidden.astype(jnp.float32), w_down[lower:lower + PIECES].astype(jnp.float32), precision=highest).astype(jnp.bfloat16)
        expert_out = lax.optimization_barrier(jnp.sum(piece_out.astype(jnp.float32), axis=1))
        mixture = mixture + selection[:, expert:expert + 1] * expert_out
    routed = mixture.reshape(HALVES, HALF_ROWS, D).astype(jnp.bfloat16)
    return jnp.stack([stream, routed])
```

```python
import jax
import jax.numpy as jnp
from jax import lax
from jax.experimental import pallas as pl
from jax.experimental.pallas import tpu as pltpu
from jax.sharding import PartitionSpec as P

D = 7168
LAT = 512
KW = 576
VH = 128
UNITS = 128
EPS = 1e-6
SCALE = 192 ** (-0.5)

NZ = 8
NP = 8
NY = 4
OWN = 8
COLS = D // NP
CHUNK = NY * OWN
ROWS = NZ * CHUNK
NH = NZ * NY
F32 = jnp.float32
BF16 = jnp.bfloat16


def kernel(
    q_ref, pool_ref, tab_ref, len_ref, wuv_ref, wout_ref, res_ref, gain_ref,
    ids_ref, gates_ref, wg_ref, wu_ref, wd_ref,
    out_ref,
    pool, wuv, gain, qbuf, lat_out, lat_in, sel, resbuf, selbuf,
    wo, wgu, wd, head_own, head_all, c_out, c_in,
    stream_out, stream_in, ssq_own, ssq_in, rs_all, x_all,
    h_out, h_in, hid_own, hid_all, o_out, o_in, mix_out, mix_in,
    load, send, recv,
):
    c = lax.axis_index("side")
    h = lax.axis_index("head")
    sub = lax.axis_index("sub")
    z, n = h // NP, h % NP
    xl, y = n // NY, n % NY
    spot = z * NY + y

    def device(core, head):
        return (core, head, sub)

    def put(src, dst, phase, core, head):
        pltpu.make_async_remote_copy(
            src_ref=src, dst_ref=dst, send_sem=send.at[phase], recv_sem=recv.at[phase],
            device_id=device(core, head), device_id_type=pl.DeviceIdType.MESH,
        ).start()

    def keep(src, dst, phase):
        pltpu.make_async_copy(src, dst, recv.at[phase]).start()

    def arrived(ref, phase):
        pltpu.make_async_copy(ref, ref, recv.at[phase]).wait()

    def gone(ref, phase):
        pltpu.make_async_copy(ref, ref, send.at[phase]).wait()

    def loop(count, body):
        def step(k, carry):
            body(k)
            return carry
        lax.fori_loop(0, count, step, 0)

    def plane(k):
        return (n + k) % NP

    def depth(k):
        return (z + k) % NZ

    def cols(m):
        return pl.ds(pl.multiple_of(m * COLS, 128), COLS)

    Q, RES, SEL, LATS, WO, WOF, HEAD, C, STREAM, SSQ, RS, X, WG, WU, WGUF, WD, WDF, H, HID, O, MIX = range(21)

    def send_query(k):
        m = (k + spot) % NH
        owner = (m // NY) * NP + c * NY + m % NY
        put(q_ref.at[owner], qbuf.at[spot], Q, 1 - xl, owner)
    loop(NH, send_query)

    pltpu.make_async_copy(pool_ref, pool, load.at[0]).start()
    pltpu.make_async_copy(wuv_ref, wuv, load.at[1]).start()
    pltpu.make_async_copy(gain_ref.at[:, cols(n)], gain, load.at[2]).start()

    lane = lax.broadcasted_iota(jnp.int32, (OWN, 128), 1)
    picked = jnp.zeros((OWN, 128), F32)
    for k in range(ids_ref.shape[1]):
        picked = picked + jnp.where(ids_ref[:, k:k + 1] == lane, gates_ref[:, k:k + 1], 0.0)
    sel[...] = picked

    def send_residual(k):
        m = (1 - c) * NY + (y + k) % NY
        put(res_ref.at[:, cols(m)], resbuf.at[y], RES, xl, z * NP + m)
        put(sel, selbuf.at[y], SEL, xl, z * NP + m)
    loop(NY, send_residual)

    half_o = pl.ds(pl.multiple_of(c * (VH // 2), VH // 2), VH // 2)
    half_d = pl.ds(pl.multiple_of(c * (UNITS // 2), UNITS // 2), UNITS // 2)
    half_g = pl.ds(pl.multiple_of(c * (COLS // 2), COLS // 2), COLS // 2)

    keep(wout_ref.at[half_o, cols(n)], wo.at[n, half_o], WO)
    def send_wo(k):
        m = plane(k + 1)
        put(wout_ref.at[half_o, cols(m)], wo.at[n, half_o], WO, c, z * NP + m)
    loop(NP - 1, send_wo)

    def depth_rows(m):
        return pl.ds(pl.multiple_of(m * COLS + c * (COLS // 2), COLS // 2), COLS // 2)

    block = lax.broadcasted_iota(jnp.int32, (OWN, 1024), 1) // 64
    offset = lax.broadcasted_iota(jnp.int32, (OWN, 1024), 1) % 64
    row = lax.broadcasted_iota(jnp.int32, (OWN, 1024), 0)
    length = jnp.zeros((OWN, 1024), jnp.int32)
    for r in range(OWN):
        length = jnp.where(row == r, len_ref[r], length)
    seen = ((block == tab_ref[:, 0:1]) & (offset < length)) | (
        (block == tab_ref[:, 1:2]) & (offset + 64 < length))
    bias = jnp.where(seen, 0.0, -1e30).astype(F32)

    pltpu.make_async_copy(pool_ref, pool, load.at[0]).wait()
    arrived(qbuf, Q)
    queries = qbuf[...].astype(F32).reshape(NH * OWN, KW).astype(BF16)
    keys = pool[...].reshape(1024, KW)
    scores = lax.dot_general(
        queries, keys, (((1,), (1,)), ((), ())), preferred_element_type=F32)
    scores = scores.reshape(NH, OWN, 1024) * SCALE + bias[None]
    scores = scores.reshape(NH * OWN, 1024)
    peak = jnp.max(scores, axis=-1, keepdims=True)
    raw = jnp.exp(scores - peak)
    total = jnp.sum(raw, axis=-1, keepdims=True)
    latents = jnp.dot(raw.astype(BF16), keys[:, :LAT], preferred_element_type=F32) / total
    lat_out[...] = latents.reshape(NH, OWN, LAT).astype(BF16)

    def send_latent(k):
        m = (k + spot) % NH
        put(lat_out.at[m], lat_in.at[spot], LATS, xl, (m // NY) * NP + (1 - c) * NY + m % NY)
    loop(NH, send_latent)

    keep(wg_ref.at[depth_rows(n)], wgu.at[n, half_g, pl.ds(0, 128)], WG)
    keep(wu_ref.at[depth_rows(n)], wgu.at[n, half_g, pl.ds(128, 128)], WU)
    def send_wgu(k):
        m = plane(k + 1)
        put(wg_ref.at[depth_rows(m)], wgu.at[n, half_g, pl.ds(0, 128)], WG, c, z * NP + m)
        put(wu_ref.at[depth_rows(m)], wgu.at[n, half_g, pl.ds(128, 128)], WU, c, z * NP + m)
    loop(NP - 1, send_wgu)

    arrived(wo.at[:, half_o], WO)
    put(wo.at[:, half_o], wo.at[:, half_o], WOF, 1 - c, h)

    pltpu.make_async_copy(wuv_ref, wuv, load.at[1]).wait()
    arrived(lat_in, LATS)
    latent_rows = lat_in[...].astype(F32).reshape(ROWS, LAT).astype(BF16)
    head_own[...] = jnp.dot(latent_rows, wuv[...], preferred_element_type=F32).astype(BF16)
    keep(head_own, head_all.at[n], HEAD)
    def send_head(k):
        put(head_own, head_all.at[n], HEAD, c, z * NP + plane(k + 1))
    loop(NP - 1, send_head)

    arrived(wo.at[:, half_o], WOF)
    arrived(head_all, HEAD)
    heads = jnp.concatenate([head_all[i] for i in range(NP)], axis=1)
    partial = jnp.dot(heads, wo[...].reshape(NP * VH, COLS), preferred_element_type=F32)
    c_out[...] = partial.astype(BF16).reshape(NZ, CHUNK, COLS)
    keep(c_out.at[z], c_in.at[z], C)
    def send_c(k):
        m = depth(k + 1)
        put(c_out.at[m], c_in.at[z], C, c, m * NP + n)
    loop(NZ - 1, send_c)

    arrived(resbuf, RES)
    arrived(selbuf, SEL)
    pltpu.make_async_copy(gain_ref.at[:, cols(n)], gain, load.at[2]).wait()
    arrived(c_in, C)
    attended = c_in[0].astype(F32)
    for i in range(1, NZ):
        attended = attended + c_in[i].astype(F32)
    stream = (resbuf[...].astype(F32).reshape(CHUNK, COLS) + attended).astype(BF16).astype(F32)
    x_all[z] = (stream * gain[...]).astype(BF16)
    def send_x(k):
        put(x_all.at[z], x_all.at[z], X, c, depth(k + 1) * NP + n)
    loop(NZ - 1, send_x)

    ssq_own[...] = jnp.broadcast_to(jnp.sum(stream * stream, axis=-1, keepdims=True), (CHUNK, 128))
    keep(ssq_own, ssq_in.at[n], SSQ)
    def send_ssq(k):
        put(ssq_own, ssq_in.at[n], SSQ, c, z * NP + plane(k + 1))
    loop(NP - 1, send_ssq)

    stream_out[...] = stream.reshape(NY, OWN, COLS).astype(BF16)

    def home(core, src, landing, phase):
        def step(k):
            own = (c == core) & (xl == c) & (y == k)
            @pl.when(own)
            def _():
                keep(src.at[k], landing.at[n], phase)
            @pl.when(jnp.logical_not(own))
            def _():
                put(src.at[k], landing.at[n], phase, core, z * NP + c * NY + k)
        loop(NY, step)

    home(0, stream_out, stream_in, STREAM)

    arrived(ssq_in, SSQ)
    square = ssq_in[0]
    for i in range(1, NP):
        square = square + ssq_in[i]
    scale = lax.rsqrt(square * (1.0 / D) + EPS)
    wide = lax.broadcasted_iota(jnp.int32, (CHUNK, 128), 1)
    rs_all[z] = jnp.where(wide < 8, selbuf[...].reshape(CHUNK, 128), scale)
    def send_rs(k):
        put(rs_all.at[z], rs_all.at[z], RS, c, depth(k + 1) * NP + n)
    loop(NZ - 1, send_rs)

    arrived(wgu.at[:, half_g, pl.ds(0, 128)], WG)
    arrived(wgu.at[:, half_g, pl.ds(128, 128)], WU)
    put(wgu.at[:, half_g], wgu.at[:, half_g], WGUF, 1 - c, h)

    keep(wd_ref.at[half_d, cols(n)], wd.at[n, half_d], WD)
    def send_wd(k):
        m = plane(k + 1)
        put(wd_ref.at[half_d, cols(m)], wd.at[n, half_d], WD, c, z * NP + m)
    loop(NP - 1, send_wd)

    arrived(x_all.at[pl.ds(0, NZ - 1)], X)
    arrived(wgu.at[:, half_g], WGUF)
    x = x_all[...].reshape(ROWS, COLS)
    def send_h(k):
        m = plane(k + 1)
        h_out[m] = jnp.dot(x, wgu[m], preferred_element_type=F32).astype(BF16)
        put(h_out.at[m], h_in.at[n], H, c, z * NP + m)
    loop(NP - 1, send_h)
    h_out[n] = jnp.dot(x, wgu[n], preferred_element_type=F32).astype(BF16)
    keep(h_out.at[n], h_in.at[n], H)

    arrived(wd.at[:, half_d], WD)
    put(wd.at[:, half_d], wd.at[:, half_d], WDF, 1 - c, h)

    arrived(rs_all.at[pl.ds(0, NZ - 1)], RS)
    tiles = rs_all[...].reshape(ROWS, 128)
    lanes = lax.broadcasted_iota(jnp.int32, (ROWS, 128), 1)
    scale = jnp.sum(jnp.where(lanes == 8, tiles, 0.0), axis=-1, keepdims=True)
    gate_of = jnp.sum(jnp.where(lanes == z, tiles, 0.0), axis=-1, keepdims=True)

    arrived(h_in, H)
    products = h_in[0].astype(F32)
    for i in range(1, NP):
        products = products + h_in[i].astype(F32)
    products = products * scale
    gated = products[:, :UNITS]
    hid_own[...] = (gated * jax.nn.sigmoid(gated) * products[:, UNITS:]).astype(BF16)
    keep(hid_own, hid_all.at[n], HID)
    def send_hid(k):
        put(hid_own, hid_all.at[n], HID, c, z * NP + plane(k + 1))
    loop(NP - 1, send_hid)

    arrived(wd.at[:, half_d], WDF)
    arrived(hid_all, HID)
    hidden = jnp.concatenate([hid_all[i] for i in range(NP)], axis=1)
    expert = jnp.dot(hidden, wd[...].reshape(NP * UNITS, COLS), preferred_element_type=F32)
    o_out[...] = (expert * gate_of).astype(BF16).reshape(NZ, CHUNK, COLS)
    keep(o_out.at[z], o_in.at[z], O)
    def send_o(k):
        m = depth(k + 1)
        put(o_out.at[m], o_in.at[z], O, c, m * NP + n)
    loop(NZ - 1, send_o)

    arrived(o_in, O)
    mixture = o_in[0].astype(F32)
    for i in range(1, NZ):
        mixture = mixture + o_in[i].astype(F32)
    mix_out[...] = mixture.reshape(NY, OWN, COLS).astype(BF16)
    home(1, mix_out, mix_in, MIX)

    def finish(landing, phase):
        arrived(landing, phase)
        for i in range(NP):
            out_ref[:, i * COLS:(i + 1) * COLS] = landing[i]

    @pl.when(c == 0)
    def _():
        finish(stream_in, STREAM)

    @pl.when(c == 1)
    def _():
        finish(mix_in, MIX)

    gone(qbuf, Q)
    gone(resbuf, RES)
    gone(selbuf, SEL)
    gone(lat_in, LATS)
    part = pl.ds(0, NP - 1)
    gone(wo.at[part, half_o], WO)
    gone(wo.at[:, half_o], WOF)
    gone(head_all.at[part], HEAD)
    gone(c_in.at[part], C)
    gone(ssq_in.at[part], SSQ)
    gone(rs_all.at[part], RS)
    gone(x_all.at[part], X)
    gone(wgu.at[part, half_g, pl.ds(0, 128)], WG)
    gone(wgu.at[part, half_g, pl.ds(128, 128)], WU)
    gone(wgu.at[:, half_g], WGUF)
    gone(wd.at[part, half_d], WD)
    gone(wd.at[:, half_d], WDF)
    gone(h_in.at[part], H)
    gone(hid_all.at[part], HID)
    gone(o_in.at[part], O)

    def gone_home(core, src, phase):
        own = (c == core) & (xl == c)
        @pl.when(own)
        def _():
            gone(src.at[pl.ds(0, NY - 1)], phase)
        @pl.when(jnp.logical_not(own))
        def _():
            gone(src, phase)

    gone_home(0, stream_out, STREAM)
    gone_home(1, mix_out, MIX)


def per_device(
    queries, cache_pool, block_table, cache_len, w_uv, w_out, residual, norm_gain,
    expert_ids, expert_gates, w_gate, w_up, w_down,
):
    hbm = pl.BlockSpec(memory_space=pl.ANY)
    vmem = pl.BlockSpec(memory_space=pltpu.VMEM)
    smem = pl.BlockSpec(memory_space=pltpu.SMEM)
    shapes = [
        ((16, 64, KW), BF16),
        ((LAT, VH), BF16),
        ((1, COLS), F32),
        ((NH, OWN, KW), BF16),
        ((NH, OWN, LAT), BF16),
        ((NH, OWN, LAT), BF16),
        ((OWN, 128), F32),
        ((NY, OWN, COLS), BF16),
        ((NY, OWN, 128), F32),
        ((NP, VH, COLS), BF16),
        ((NP, COLS, 2 * UNITS), BF16),
        ((NP, UNITS, COLS), BF16),
        ((ROWS, VH), BF16),
        ((NP, ROWS, VH), BF16),
        ((NZ, CHUNK, COLS), BF16),
        ((NZ, CHUNK, COLS), BF16),
        ((NY, OWN, COLS), BF16),
        ((NP, OWN, COLS), BF16),
        ((CHUNK, 128), F32),
        ((NP, CHUNK, 128), F32),
        ((NZ, CHUNK, 128), F32),
        ((NZ, CHUNK, COLS), BF16),
        ((NP, ROWS, 2 * UNITS), BF16),
        ((NP, ROWS, 2 * UNITS), BF16),
        ((ROWS, UNITS), BF16),
        ((NP, ROWS, UNITS), BF16),
        ((NZ, CHUNK, COLS), BF16),
        ((NZ, CHUNK, COLS), BF16),
        ((NY, OWN, COLS), BF16),
        ((NP, OWN, COLS), BF16),
    ]
    result = pl.pallas_call(
        kernel,
        out_shape=jax.ShapeDtypeStruct((OWN, D), BF16),
        in_specs=[hbm, hbm, vmem, smem, hbm, hbm, hbm, hbm, vmem, vmem, hbm, hbm, hbm],
        out_specs=vmem,
        scratch_shapes=[pltpu.VMEM(shape, dtype) for shape, dtype in shapes] + [
            pltpu.SemaphoreType.DMA((3,)),
            pltpu.SemaphoreType.DMA((21,)),
            pltpu.SemaphoreType.DMA((21,)),
        ],
        compiler_params=pltpu.CompilerParams(
            has_side_effects=True, vmem_limit_bytes=44 * 1024 * 1024),
        cost_estimate=pl.CostEstimate(
            flops=4_000_000_000, bytes_accessed=16_000_000, transcendentals=400_000),
        name="layer",
    )(
        queries.reshape(64, OWN, KW), cache_pool[0], block_table[0], cache_len[0],
        w_uv[0], w_out[0], residual[0], norm_gain.reshape(1, D),
        expert_ids[0], expert_gates[0], w_gate[0], w_up[0], w_down[0],
    )
    return result[None, None]


def solution(mesh):
    in_specs = (
        P("sub", None, "head", None),
        P("sub", "head", None, None),
        P("sub", "head", None),
        P("sub", "head"),
        P("head", None, None),
        P("head", None, None),
        P("sub", "head", None),
        P(),
        P("sub", "head", None),
        P("sub", "head", None),
        P("head", None, None),
        P("head", None, None),
        P("head", None, None),
    )
    out_specs = P("side", "sub", "head", None)
    return jax.shard_map(
        per_device, mesh=mesh, in_specs=in_specs, out_specs=out_specs, check_vma=False
    )
```

```python
import jax
import jax.numpy as jnp
from jax import lax
from jax.experimental import pallas as pl
from jax.experimental.pallas import tpu as pltpu
from jax.sharding import PartitionSpec as P

D = 7168
LAT = 512
KW = 576
VH = 128
UNITS = 128
EPS = 1e-6
SCALE = 192 ** (-0.5)

NZ = 8
NP = 8
NY = 4
OWN = 8
COLS = D // NP
CHUNK = NY * OWN
ROWS = NZ * CHUNK
NH = NZ * NY
HB = 2
PART = ROWS // HB
STRIP = CHUNK // HB
MEET = 2 * NH + 2 * NP - 1 + NZ - 1
F32 = jnp.float32
BF16 = jnp.bfloat16


NAMES = (
    ["Q", "RES", "SEL", "LATS", "WO", "WOF", "WG", "WGF", "WU", "WUF", "WD", "WDF", "STREAM", "MIX"]
    + [name + str(b) for name in ("HEAD", "C", "SSQ", "RS", "X", "H", "HID", "O") for b in range(HB)]
)
PHASE = {name: i for i, name in enumerate(NAMES)}


def kernel(
    q_ref, pool_ref, tab_ref, len_ref, wuv_ref, wout_ref, res_ref, gain_ref,
    ids_ref, gates_ref, wg_ref, wu_ref, wd_ref,
    out_ref,
    qcols, qrows, pool, wuv, gain, qbuf, lat_out, lat_in, sel, resbuf, selbuf,
    wo, wgu, wd, head_own, head_all, c_out, c_in,
    stream_out, stream_in, ssq_own, ssq_in, rs_all, x_all,
    h_out, h_in, hid_own, hid_all, o_out, o_in, mix_out, mix_in,
    load, send, recv,
):
    c = lax.axis_index("side")
    h = lax.axis_index("head")
    sub = lax.axis_index("sub")
    z, n = h // NP, h % NP
    xl, y = n // NY, n % NY
    spot = z * NY + y

    def device(core, head):
        return (core, head, sub)

    def put(src, dst, phase, core, head):
        pltpu.make_async_remote_copy(
            src_ref=src, dst_ref=dst,
            send_sem=send.at[PHASE[phase]], recv_sem=recv.at[PHASE[phase]],
            device_id=device(core, head), device_id_type=pl.DeviceIdType.MESH,
        ).start()

    def keep(src, dst, phase):
        pltpu.make_async_copy(src, dst, recv.at[PHASE[phase]]).start()

    def arrived(ref, phase):
        with jax.named_scope("w_" + phase):
            pltpu.make_async_copy(ref, ref, recv.at[PHASE[phase]]).wait()

    def gone(ref, phase):
        pltpu.make_async_copy(ref, ref, send.at[PHASE[phase]]).wait()

    def loop(count, body):
        def step(k, carry):
            body(k)
            return carry
        lax.fori_loop(0, count, step, 0)

    def plane(k):
        return (n + k) % NP

    def depth(k):
        return (z + k) % NZ

    def cols(m):
        return pl.ds(pl.multiple_of(m * COLS, 128), COLS)

    loads = [
        pltpu.make_async_copy(q_ref, qcols, load.at[0]),
        pltpu.make_async_copy(pool_ref, pool, load.at[1]),
        pltpu.make_async_copy(wuv_ref, wuv, load.at[2]),
        pltpu.make_async_copy(gain_ref.at[:, cols(n)], gain, load.at[3]),
    ]
    for copy in loads:
        copy.start()

    barrier = pltpu.get_barrier_semaphore()

    def greet(core, head):
        pl.semaphore_signal(
            barrier, inc=1, device_id=device(core, head), device_id_type=pl.DeviceIdType.MESH)

    def greet_far(k):
        m = (k + spot) % NH
        greet(1 - xl, (m // NY) * NP + c * NY + m % NY)
        greet(xl, (m // NY) * NP + (1 - c) * NY + m % NY)
    loop(NH, greet_far)

    def greet_plane(k):
        m = (c * NP + n + k + 1) % (2 * NP)
        greet(m // NP, z * NP + m % NP)
    loop(2 * NP - 1, greet_plane)

    def greet_depth(k):
        greet(c, depth(k + 1) * NP + n)
    loop(NZ - 1, greet_depth)

    loads[0].wait()
    for i in range(0, KW, 128):
        wide = min(128, KW - i)
        turned = jnp.transpose(qcols[i:i + wide, :].astype(F32))
        qrows[:, :, i:i + wide] = turned.reshape(64, OWN, wide).astype(BF16)

    lane = lax.broadcasted_iota(jnp.int32, (OWN, 128), 1)
    line = lax.broadcasted_iota(jnp.int32, (OWN, 128), 0)
    picked = jnp.zeros((OWN, 128), F32)
    for r in range(OWN):
        for k in range(ids_ref.shape[0]):
            picked = picked + jnp.where((line == r) & (lane == ids_ref[k, r]), gates_ref[k, r], 0.0)
    sel[...] = picked

    row = lax.broadcasted_iota(jnp.int32, (OWN, 1024), 0)
    place = lax.broadcasted_iota(jnp.int32, (OWN, 1024), 1)
    block, offset = place // 64, place % 64
    bias = jnp.full((OWN, 1024), -1e30, F32)
    for r in range(OWN):
        seen = ((block == tab_ref[0, r]) & (offset < len_ref[0, r])) | (
            (block == tab_ref[1, r]) & (offset + 64 < len_ref[0, r]))
        bias = jnp.where((row == r) & seen, 0.0, bias)

    with jax.named_scope("w_barrier"):
        pl.semaphore_wait(barrier, MEET)

    def send_query(k):
        m = (k + spot) % NH
        owner = (m // NY) * NP + c * NY + m % NY
        put(qrows.at[owner], qbuf.at[spot], "Q", 1 - xl, owner)
    loop(NH, send_query)

    def send_residual(k):
        m = (1 - c) * NY + (y + k) % NY
        put(res_ref.at[:, cols(m)], resbuf.at[y], "RES", xl, z * NP + m)
        put(sel, selbuf.at[y], "SEL", xl, z * NP + m)
    loop(NY, send_residual)

    half = pl.ds(pl.multiple_of(c * 64, 64), 64)
    half_g = pl.ds(pl.multiple_of(c * (COLS // 2), COLS // 2), COLS // 2)
    left, right = pl.ds(0, UNITS), pl.ds(UNITS, UNITS)

    def depth_rows(m):
        return pl.ds(pl.multiple_of(m * COLS + c * (COLS // 2), COLS // 2), COLS // 2)

    def share(source, landing, phase):
        keep(source(n), landing, phase)
        def step(k):
            m = plane(k + 1)
            put(source(m), landing, phase, c, z * NP + m)
        loop(NP - 1, step)

    share(lambda m: wout_ref.at[half, cols(m)], wo.at[n, half], "WO")

    loads[1].wait()
    arrived(qbuf, "Q")
    queries = qbuf[...].astype(F32).reshape(NH * OWN, KW).astype(BF16)
    keys = pool[...].reshape(1024, KW)
    scores = lax.dot_general(
        queries, keys, (((1,), (1,)), ((), ())), preferred_element_type=F32)
    scores = scores.reshape(NH, OWN, 1024) * SCALE + bias[None]
    scores = scores.reshape(NH * OWN, 1024)
    peak = jnp.max(scores, axis=-1, keepdims=True)
    raw = jnp.exp(scores - peak)
    total = jnp.sum(raw, axis=-1, keepdims=True)
    latents = jnp.dot(raw.astype(BF16), keys[:, :LAT], preferred_element_type=F32) / total
    lat_out[...] = latents.reshape(NH, OWN, LAT).astype(BF16)

    def send_latent(k):
        m = (k + spot) % NH
        put(lat_out.at[m], lat_in.at[y // 2, z, y % 2], "LATS",
            xl, (m // NY) * NP + (1 - c) * NY + m % NY)
    loop(NH, send_latent)

    share(lambda m: wg_ref.at[depth_rows(m)], wgu.at[n, half_g, left], "WG")

    arrived(wo.at[:, half], "WO")
    put(wo.at[:, half], wo.at[:, half], "WOF", 1 - c, h)

    loads[2].wait()
    arrived(lat_in, "LATS")
    for b in range(HB):
        rows = lat_in[b].astype(F32).reshape(PART, LAT).astype(BF16)
        head_own[b] = jnp.dot(rows, wuv[...], preferred_element_type=F32).astype(BF16)
        keep(head_own.at[b], head_all.at[b, n], f"HEAD{b}")
        def send_head(k):
            put(head_own.at[b], head_all.at[b, n], f"HEAD{b}", c, z * NP + plane(k + 1))
        loop(NP - 1, send_head)

    arrived(wo.at[:, half], "WOF")
    for b in range(HB):
        arrived(head_all.at[b], f"HEAD{b}")
        heads = jnp.concatenate([head_all[b, i] for i in range(NP)], axis=1)
        partial = jnp.dot(heads, wo[...].reshape(NP * VH, COLS), preferred_element_type=F32)
        c_out[b] = partial.astype(BF16).reshape(NZ, STRIP, COLS)
        keep(c_out.at[b, z], c_in.at[b, z], f"C{b}")
        def send_c(k):
            m = depth(k + 1)
            put(c_out.at[b, m], c_in.at[b, z], f"C{b}", c, m * NP + n)
        loop(NZ - 1, send_c)

    share(lambda m: wu_ref.at[depth_rows(m)], wgu.at[n, half_g, right], "WU")
    share(lambda m: wd_ref.at[half, cols(m)], wd.at[n, half], "WD")
    arrived(wgu.at[:, half_g, left], "WG")
    put(wgu.at[:, half_g, left], wgu.at[:, half_g, left], "WGF", 1 - c, h)

    def home(core, src, landing, phase, k):
        own = (c == core) & (xl == c) & (y == k)
        @pl.when(own)
        def _():
            keep(src.at[k], landing.at[n], phase)
        @pl.when(jnp.logical_not(own))
        def _():
            put(src.at[k], landing.at[n], phase, core, z * NP + c * NY + k)

    arrived(resbuf, "RES")
    arrived(selbuf, "SEL")
    loads[3].wait()
    for b in range(HB):
        pair = slice(2 * b, 2 * b + 2)
        arrived(c_in.at[b], f"C{b}")
        attended = c_in[b, 0].astype(F32)
        for i in range(1, NZ):
            attended = attended + c_in[b, i].astype(F32)
        residual = resbuf[pair].astype(F32).reshape(STRIP, COLS)
        stream = (residual + attended).astype(BF16).astype(F32)
        x_all[b, z] = (stream * gain[...]).astype(BF16)
        def send_x(k):
            put(x_all.at[b, z], x_all.at[b, z], f"X{b}", c, depth(k + 1) * NP + n)
        loop(NZ - 1, send_x)

        squares = jnp.sum(stream * stream, axis=-1, keepdims=True)
        ssq_own[b] = jnp.broadcast_to(squares, (STRIP, 128))
        keep(ssq_own.at[b], ssq_in.at[b, n], f"SSQ{b}")
        def send_ssq(k):
            put(ssq_own.at[b], ssq_in.at[b, n], f"SSQ{b}", c, z * NP + plane(k + 1))
        loop(NP - 1, send_ssq)

        stream_out[pair] = stream.reshape(2, OWN, COLS).astype(BF16)
        home(0, stream_out, stream_in, "STREAM", 2 * b)
        home(0, stream_out, stream_in, "STREAM", 2 * b + 1)

    for b in range(HB):
        arrived(ssq_in.at[b], f"SSQ{b}")
        square = ssq_in[b, 0]
        for i in range(1, NP):
            square = square + ssq_in[b, i]
        scale = lax.rsqrt(square * (1.0 / D) + EPS)
        wide = lax.broadcasted_iota(jnp.int32, (STRIP, 128), 1)
        chosen = selbuf[2 * b:2 * b + 2].reshape(STRIP, 128)
        rs_all[b, z] = jnp.where(wide < 8, chosen, scale)
        def send_rs(k):
            put(rs_all.at[b, z], rs_all.at[b, z], f"RS{b}", c, depth(k + 1) * NP + n)
        loop(NZ - 1, send_rs)

    arrived(wgu.at[:, half_g, right], "WU")
    put(wgu.at[:, half_g, right], wgu.at[:, half_g, right], "WUF", 1 - c, h)

    arrived(wgu.at[:, half_g, left], "WGF")
    arrived(wgu.at[:, half_g, right], "WUF")
    others = pl.ds(0, NP - 1)
    for b in range(HB):
        arrived(x_all.at[b, others], f"X{b}")
        x = x_all[b].reshape(PART, COLS)
        def send_h(k):
            m = plane(k + 1)
            h_out[b, m] = jnp.dot(x, wgu[m], preferred_element_type=F32).astype(BF16)
            put(h_out.at[b, m], h_in.at[b, n], f"H{b}", c, z * NP + m)
        loop(NP - 1, send_h)
        h_out[b, n] = jnp.dot(x, wgu[n], preferred_element_type=F32).astype(BF16)
        keep(h_out.at[b, n], h_in.at[b, n], f"H{b}")

    arrived(wd.at[:, half], "WD")
    put(wd.at[:, half], wd.at[:, half], "WDF", 1 - c, h)

    lanes = lax.broadcasted_iota(jnp.int32, (PART, 128), 1)
    gate_of = []
    for b in range(HB):
        arrived(rs_all.at[b, others], f"RS{b}")
        tiles = rs_all[b].reshape(PART, 128)
        scale = jnp.sum(jnp.where(lanes == 8, tiles, 0.0), axis=-1, keepdims=True)
        gate_of.append(jnp.sum(jnp.where(lanes == z, tiles, 0.0), axis=-1, keepdims=True))

        arrived(h_in.at[b], f"H{b}")
        products = h_in[b, 0].astype(F32)
        for i in range(1, NP):
            products = products + h_in[b, i].astype(F32)
        products = products * scale
        gated = products[:, :UNITS]
        hid_own[b] = (gated * jax.nn.sigmoid(gated) * products[:, UNITS:]).astype(BF16)
        keep(hid_own.at[b], hid_all.at[b, n], f"HID{b}")
        def send_hid(k):
            put(hid_own.at[b], hid_all.at[b, n], f"HID{b}", c, z * NP + plane(k + 1))
        loop(NP - 1, send_hid)

    arrived(wd.at[:, half], "WDF")
    for b in range(HB):
        arrived(hid_all.at[b], f"HID{b}")
        hidden = jnp.concatenate([hid_all[b, i] for i in range(NP)], axis=1)
        expert = jnp.dot(hidden, wd[...].reshape(NP * UNITS, COLS), preferred_element_type=F32)
        o_out[b] = (expert * gate_of[b]).astype(BF16).reshape(NZ, STRIP, COLS)
        keep(o_out.at[b, z], o_in.at[b, z], f"O{b}")
        def send_o(k):
            m = depth(k + 1)
            put(o_out.at[b, m], o_in.at[b, z], f"O{b}", c, m * NP + n)
        loop(NZ - 1, send_o)

    for b in range(HB):
        arrived(o_in.at[b], f"O{b}")
        mixture = o_in[b, 0].astype(F32)
        for i in range(1, NZ):
            mixture = mixture + o_in[b, i].astype(F32)
        mix_out[2 * b:2 * b + 2] = mixture.reshape(2, OWN, COLS).astype(BF16)
        home(1, mix_out, mix_in, "MIX", 2 * b)
        home(1, mix_out, mix_in, "MIX", 2 * b + 1)

    def finish(landing, phase):
        arrived(landing, phase)
        for i in range(NP):
            out_ref[:, i * COLS:(i + 1) * COLS] = landing[i]

    @pl.when(c == 0)
    def _():
        finish(stream_in, "STREAM")

    @pl.when(c == 1)
    def _():
        finish(mix_in, "MIX")

    gone(qbuf, "Q")
    gone(resbuf, "RES")
    gone(selbuf, "SEL")
    gone(lat_in, "LATS")
    gone(wo.at[others, half], "WO")
    gone(wo.at[:, half], "WOF")
    gone(wgu.at[others, half_g, left], "WG")
    gone(wgu.at[:, half_g, left], "WGF")
    gone(wgu.at[others, half_g, right], "WU")
    gone(wgu.at[:, half_g, right], "WUF")
    gone(wd.at[others, half], "WD")
    gone(wd.at[:, half], "WDF")
    for b in range(HB):
        gone(head_all.at[b, others], f"HEAD{b}")
        gone(c_in.at[b, others], f"C{b}")
        gone(ssq_in.at[b, others], f"SSQ{b}")
        gone(rs_all.at[b, others], f"RS{b}")
        gone(x_all.at[b, others], f"X{b}")
        gone(h_in.at[b, others], f"H{b}")
        gone(hid_all.at[b, others], f"HID{b}")
        gone(o_in.at[b, others], f"O{b}")

    def gone_home(core, src, phase):
        own = (c == core) & (xl == c)
        @pl.when(own)
        def _():
            gone(src.at[pl.ds(0, NY - 1)], phase)
        @pl.when(jnp.logical_not(own))
        def _():
            gone(src, phase)

    gone_home(0, stream_out, "STREAM")
    gone_home(1, mix_out, "MIX")


def per_device(
    queries, cache_pool, block_table, cache_len, w_uv, w_out, residual, norm_gain,
    expert_ids, expert_gates, w_gate, w_up, w_down,
):
    hbm = pl.BlockSpec(memory_space=pl.ANY)
    smem = pl.BlockSpec(memory_space=pltpu.SMEM)
    shapes = [
        ((KW, 512), BF16),
        ((64, OWN, KW), BF16),
        ((16, 64, KW), BF16),
        ((LAT, VH), BF16),
        ((1, COLS), F32),
        ((NH, OWN, KW), BF16),
        ((NH, OWN, LAT), BF16),
        ((HB, NZ, 2, OWN, LAT), BF16),
        ((OWN, 128), F32),
        ((NY, OWN, COLS), BF16),
        ((NY, OWN, 128), F32),
        ((NP, VH, COLS), BF16),
        ((NP, COLS, 2 * UNITS), BF16),
        ((NP, UNITS, COLS), BF16),
        ((HB, PART, VH), BF16),
        ((HB, NP, PART, VH), BF16),
        ((HB, NZ, STRIP, COLS), BF16),
        ((HB, NZ, STRIP, COLS), BF16),
        ((NY, OWN, COLS), BF16),
        ((NP, OWN, COLS), BF16),
        ((HB, STRIP, 128), F32),
        ((HB, NP, STRIP, 128), F32),
        ((HB, NZ, STRIP, 128), F32),
        ((HB, NZ, STRIP, COLS), BF16),
        ((HB, NP, PART, 2 * UNITS), BF16),
        ((HB, NP, PART, 2 * UNITS), BF16),
        ((HB, PART, UNITS), BF16),
        ((HB, NP, PART, UNITS), BF16),
        ((HB, NZ, STRIP, COLS), BF16),
        ((HB, NZ, STRIP, COLS), BF16),
        ((NY, OWN, COLS), BF16),
        ((NP, OWN, COLS), BF16),
    ]
    result = pl.pallas_call(
        kernel,
        out_shape=jax.ShapeDtypeStruct((OWN, D), BF16),
        in_specs=[hbm, hbm, smem, smem, hbm, hbm, hbm, hbm, smem, smem, hbm, hbm, hbm],
        out_specs=pl.BlockSpec(memory_space=pltpu.VMEM),
        scratch_shapes=[pltpu.VMEM(shape, dtype) for shape, dtype in shapes] + [
            pltpu.SemaphoreType.DMA((4,)),
            pltpu.SemaphoreType.DMA((len(NAMES),)),
            pltpu.SemaphoreType.DMA((len(NAMES),)),
        ],
        compiler_params=pltpu.CompilerParams(
            collective_id=0, has_side_effects=True, vmem_limit_bytes=60 * 1024 * 1024),
        cost_estimate=pl.CostEstimate(
            flops=4_000_000_000, bytes_accessed=16_000_000, transcendentals=400_000),
        name="layer",
    )(
        queries[0, :, 0, :].T, cache_pool[0], block_table[0].T, cache_len,
        w_uv[0], w_out[0], residual[0], norm_gain.reshape(1, D),
        expert_ids[0].T, expert_gates[0].T, w_gate[0], w_up[0], w_down[0],
    )
    return result[None, None]


def solution(mesh):
    in_specs = (
        P("sub", None, "head", None),
        P("sub", "head", None, None),
        P("sub", "head", None),
        P("sub", "head"),
        P("head", None, None),
        P("head", None, None),
        P("sub", "head", None),
        P(),
        P("sub", "head", None),
        P("sub", "head", None),
        P("head", None, None),
        P("head", None, None),
        P("head", None, None),
    )
    out_specs = P("side", "sub", "head", None)
    return jax.shard_map(
        per_device, mesh=mesh, in_specs=in_specs, out_specs=out_specs, check_vma=False
    )
```

```python
import jax
import jax.numpy as jnp
from jax import lax
from jax.experimental import pallas as pl
from jax.experimental.pallas import tpu as pltpu
from jax.sharding import PartitionSpec as P

D = 7168
LAT = 512
KW = 576
VH = 128
UNITS = 128
EPS = 1e-6
SCALE = 192 ** (-0.5)

NZ = 8
NP = 8
NY = 4
OWN = 8
COLS = D // NP
CHUNK = NY * OWN
ROWS = NZ * CHUNK
NH = NZ * NY
HB = 2
PART = ROWS // HB
STRIP = CHUNK // HB
MEET = 2 * NH + 2 * NP - 1 + NZ - 1
F32 = jnp.float32
BF16 = jnp.bfloat16


NAMES = (
    ["Q", "RES", "SEL", "LATS", "WO", "WOF", "WG", "WGF", "WU", "WUF", "WD", "WDF", "STREAM", "MIX"]
    + [name + str(b) for name in ("HEAD", "C", "SIDE", "SQ", "X", "H", "HID", "O") for b in range(HB)]
)
PHASE = {name: i for i, name in enumerate(NAMES)}


def kernel(
    q_ref, pool_ref, tab_ref, len_ref, wuv_ref, wout_ref, res_ref, gain_ref,
    ids_ref, gates_ref, wg_ref, wu_ref, wd_ref,
    out_ref,
    qcols, qrows, pool, wuv, gain, qbuf, lat_out, lat_in, sel, resbuf, selbuf,
    wo, wgu, wd, head_own, head_all, c_out, c_in,
    stream_out, stream_in, side_all, sq_own, sq_in, x_all,
    h_out, h_in, hid_own, hid_all, o_out, o_in, mix_out, mix_in,
    load, send, recv,
):
    c = lax.axis_index("side")
    h = lax.axis_index("head")
    sub = lax.axis_index("sub")
    z, n = h // NP, h % NP
    xl, y = n // NY, n % NY
    spot = z * NY + y

    def device(core, head):
        return (core, head, sub)

    def put(src, dst, phase, core, head):
        pltpu.make_async_remote_copy(
            src_ref=src, dst_ref=dst,
            send_sem=send.at[PHASE[phase]], recv_sem=recv.at[PHASE[phase]],
            device_id=device(core, head), device_id_type=pl.DeviceIdType.MESH,
        ).start()

    def keep(src, dst, phase):
        pltpu.make_async_copy(src, dst, recv.at[PHASE[phase]]).start()

    def arrived(ref, phase):
        with jax.named_scope("w_" + phase):
            pltpu.make_async_copy(ref, ref, recv.at[PHASE[phase]]).wait()

    def gone(ref, phase):
        pltpu.make_async_copy(ref, ref, send.at[PHASE[phase]]).wait()

    def loop(count, body):
        def step(k, carry):
            body(k)
            return carry
        lax.fori_loop(0, count, step, 0)

    def around(k, me, size):
        far = (k + 1) // 2
        return (me + size + far * (2 * (k % 2) - 1)) % size

    def depth(k):
        return around(k + 1, z, NZ)

    def plane(k):
        turn = jnp.where(k < 4, 1 + 2 * (k % 2), jnp.where(k == 4, 0, 2))
        flip = jnp.where(k < 4, k // 2, jnp.where(k == 5, 0, 1))
        return ((xl + flip) % 2) * NY + (y + turn) % NY

    def cols(m):
        return pl.ds(pl.multiple_of(m * COLS, 128), COLS)

    loads = [
        pltpu.make_async_copy(q_ref, qcols, load.at[0]),
        pltpu.make_async_copy(pool_ref, pool, load.at[1]),
        pltpu.make_async_copy(wuv_ref, wuv, load.at[2]),
        pltpu.make_async_copy(gain_ref.at[:, cols(n)], gain, load.at[3]),
    ]
    for copy in loads:
        copy.start()

    barrier = pltpu.get_barrier_semaphore()

    def greet(core, head):
        pl.semaphore_signal(
            barrier, inc=1, device_id=device(core, head), device_id_type=pl.DeviceIdType.MESH)

    def greet_far(k):
        m = around(k, spot, NH)
        greet(1 - xl, (m // NY) * NP + c * NY + m % NY)
        greet(xl, (m // NY) * NP + (1 - c) * NY + m % NY)
    loop(NH, greet_far)

    def greet_plane(k):
        m = (c * NP + n + k + 1) % (2 * NP)
        greet(m // NP, z * NP + m % NP)
    loop(2 * NP - 1, greet_plane)

    def greet_depth(k):
        greet(c, depth(k) * NP + n)
    loop(NZ - 1, greet_depth)

    loads[0].wait()
    for i in range(0, KW, 128):
        wide = min(128, KW - i)
        turned = jnp.transpose(qcols[i:i + wide, :].astype(F32))
        qrows[:, :, i:i + wide] = turned.reshape(64, OWN, wide).astype(BF16)

    lane = lax.broadcasted_iota(jnp.int32, (OWN, 128), 1)
    line = lax.broadcasted_iota(jnp.int32, (OWN, 128), 0)
    picked = jnp.zeros((OWN, 128), F32)
    for r in range(OWN):
        for k in range(ids_ref.shape[0]):
            picked = picked + jnp.where((line == r) & (lane == ids_ref[k, r]), gates_ref[k, r], 0.0)
    sel[...] = picked

    row = lax.broadcasted_iota(jnp.int32, (OWN, 1024), 0)
    place = lax.broadcasted_iota(jnp.int32, (OWN, 1024), 1)
    block, offset = place // 64, place % 64
    bias = jnp.full((OWN, 1024), -1e30, F32)
    for r in range(OWN):
        seen = ((block == tab_ref[0, r]) & (offset < len_ref[0, r])) | (
            (block == tab_ref[1, r]) & (offset + 64 < len_ref[0, r]))
        bias = jnp.where((row == r) & seen, 0.0, bias)

    with jax.named_scope("w_barrier"):
        pl.semaphore_wait(barrier, MEET)

    def send_query(k):
        m = around(k, spot, NH)
        owner = (m // NY) * NP + c * NY + m % NY
        put(qrows.at[owner], qbuf.at[spot], "Q", 1 - xl, owner)
    loop(NH, send_query)

    def send_residual(k):
        m = (1 - c) * NY + (y + k) % NY
        put(res_ref.at[:, cols(m)], resbuf.at[y], "RES", xl, z * NP + m)
        put(sel, selbuf.at[y], "SEL", xl, z * NP + m)
    loop(NY, send_residual)

    half = pl.ds(pl.multiple_of(c * 64, 64), 64)
    half_g = pl.ds(pl.multiple_of(c * (COLS // 2), COLS // 2), COLS // 2)
    left, right = pl.ds(0, UNITS), pl.ds(UNITS, UNITS)

    def depth_rows(m):
        return pl.ds(pl.multiple_of(m * COLS + c * (COLS // 2), COLS // 2), COLS // 2)

    def share(source, landing, phase):
        keep(source(n), landing, phase)
        def step(k):
            m = plane(k)
            put(source(m), landing, phase, c, z * NP + m)
        loop(NP - 1, step)

    share(lambda m: wout_ref.at[half, cols(m)], wo.at[n, half], "WO")

    loads[1].wait()
    arrived(qbuf, "Q")
    queries = qbuf[...].astype(F32).reshape(NH * OWN, KW).astype(BF16)
    keys = pool[...].reshape(1024, KW)
    scores = lax.dot_general(
        queries, keys, (((1,), (1,)), ((), ())), preferred_element_type=F32)
    scores = scores.reshape(NH, OWN, 1024) * SCALE + bias[None]
    scores = scores.reshape(NH * OWN, 1024)
    peak = jnp.max(scores, axis=-1, keepdims=True)
    raw = jnp.exp(scores - peak)
    total = jnp.sum(raw, axis=-1, keepdims=True)
    high = raw.astype(BF16)
    low = (raw - high.astype(F32)).astype(BF16)
    values = keys[:, :LAT]
    latents = jnp.dot(high, values, preferred_element_type=F32)
    latents = (latents + jnp.dot(low, values, preferred_element_type=F32)) / total
    lat_out[...] = latents.reshape(NH, OWN, LAT).astype(BF16)

    def send_latent(k):
        m = around(k, spot, NH)
        put(lat_out.at[m], lat_in.at[y // 2, z, y % 2], "LATS",
            xl, (m // NY) * NP + (1 - c) * NY + m % NY)
    loop(NH, send_latent)


    arrived(wo.at[:, half], "WO")
    put(wo.at[:, half], wo.at[:, half], "WOF", 1 - c, h)

    loads[2].wait()
    arrived(lat_in, "LATS")
    for b in range(HB):
        rows = lat_in[b].astype(F32).reshape(PART, LAT).astype(BF16)
        head_own[b] = jnp.dot(rows, wuv[...], preferred_element_type=F32).astype(BF16)
        keep(head_own.at[b], head_all.at[b, n], f"HEAD{b}")
        def send_head(k):
            put(head_own.at[b], head_all.at[b, n], f"HEAD{b}", c, z * NP + plane(k))
        loop(NP - 1, send_head)

    share(lambda m: wg_ref.at[depth_rows(m)], wgu.at[n, half_g, left], "WG")
    share(lambda m: wu_ref.at[depth_rows(m)], wgu.at[n, half_g, right], "WU")
    arrived(wo.at[:, half], "WOF")
    for b in range(HB):
        arrived(head_all.at[b], f"HEAD{b}")
        heads = jnp.concatenate([head_all[b, i] for i in range(NP)], axis=1)
        partial = jnp.dot(heads, wo[...].reshape(NP * VH, COLS), preferred_element_type=F32)
        c_out[b] = partial.astype(BF16).reshape(NZ, STRIP, COLS)
        keep(c_out.at[b, z], c_in.at[b, z], f"C{b}")
        def send_c(k):
            m = depth(k)
            put(c_out.at[b, m], c_in.at[b, z], f"C{b}", c, m * NP + n)
        loop(NZ - 1, send_c)

    share(lambda m: wd_ref.at[half, cols(m)], wd.at[n, half], "WD")

    def home(core, src, landing, phase, k):
        own = (c == core) & (xl == c) & (y == k)
        @pl.when(own)
        def _():
            keep(src.at[k], landing.at[n], phase)
        @pl.when(jnp.logical_not(own))
        def _():
            put(src.at[k], landing.at[n], phase, core, z * NP + c * NY + k)

    arrived(resbuf, "RES")
    arrived(selbuf, "SEL")
    loads[3].wait()
    for b in range(HB):
        pair = slice(2 * b, 2 * b + 2)
        arrived(c_in.at[b], f"C{b}")
        attended = c_in[b, 0].astype(F32)
        for i in range(1, NZ):
            attended = attended + c_in[b, i].astype(F32)
        residual = resbuf[pair].astype(F32).reshape(STRIP, COLS)
        stream = (residual + attended).astype(BF16).astype(F32)
        x_all[b, z] = (stream * gain[...]).astype(BF16)
        def send_x(k):
            put(x_all.at[b, z], x_all.at[b, z], f"X{b}", c, depth(k) * NP + n)
        loop(NZ - 1, send_x)

        squares = jnp.sum(stream * stream, axis=-1, keepdims=True)
        wide = lax.broadcasted_iota(jnp.int32, (STRIP, 128), 1)
        chosen = selbuf[pair].reshape(STRIP, 128)
        side_all[b, z] = jnp.where(wide < 8, chosen, squares)
        def send_side(k):
            put(side_all.at[b, z], side_all.at[b, z], f"SIDE{b}", c, depth(k) * NP + n)
        loop(NZ - 1, send_side)

        stream_out[pair] = stream.reshape(2, OWN, COLS).astype(BF16)
        home(0, stream_out, stream_in, "STREAM", 2 * b)
        home(0, stream_out, stream_in, "STREAM", 2 * b + 1)

    arrived(wgu.at[:, half_g, left], "WG")
    put(wgu.at[:, half_g, left], wgu.at[:, half_g, left], "WGF", 1 - c, h)
    arrived(wgu.at[:, half_g, right], "WU")
    put(wgu.at[:, half_g, right], wgu.at[:, half_g, right], "WUF", 1 - c, h)

    arrived(wgu.at[:, half_g, left], "WGF")
    arrived(wgu.at[:, half_g, right], "WUF")
    others = pl.ds(0, NP - 1)
    lanes = lax.broadcasted_iota(jnp.int32, (PART, 128), 1)
    gate_of = []
    for b in range(HB):
        arrived(side_all.at[b, others], f"SIDE{b}")
        tiles = side_all[b].reshape(PART, 128)
        gate_of.append(jnp.sum(jnp.where(lanes == z, tiles, 0.0), axis=-1, keepdims=True))
        sq_own[b] = jnp.transpose(tiles)[8:16]
        keep(sq_own.at[b], sq_in.at[b, n], f"SQ{b}")
        def send_sq(k):
            put(sq_own.at[b], sq_in.at[b, n], f"SQ{b}", c, z * NP + plane(k))
        loop(NP - 1, send_sq)

        arrived(x_all.at[b, others], f"X{b}")
        x = x_all[b].reshape(PART, COLS)
        def send_h(k):
            m = plane(k)
            h_out[b, m] = jnp.dot(x, wgu[m], preferred_element_type=F32).astype(BF16)
            put(h_out.at[b, m], h_in.at[b, n], f"H{b}", c, z * NP + m)
        loop(NP - 1, send_h)
        h_out[b, n] = jnp.dot(x, wgu[n], preferred_element_type=F32).astype(BF16)
        keep(h_out.at[b, n], h_in.at[b, n], f"H{b}")

    arrived(wd.at[:, half], "WD")
    put(wd.at[:, half], wd.at[:, half], "WDF", 1 - c, h)

    for b in range(HB):
        arrived(sq_in.at[b], f"SQ{b}")
        square = sq_in[b, 0]
        for i in range(1, NP):
            square = square + sq_in[b, i]
        scale = lax.rsqrt(square * (1.0 / D) + EPS)
        scale = jnp.transpose(jnp.broadcast_to(scale[0:1], (128, PART)))

        arrived(h_in.at[b], f"H{b}")
        products = h_in[b, 0].astype(F32)
        for i in range(1, NP):
            products = products + h_in[b, i].astype(F32)
        gated = products[:, :UNITS] * scale
        lifted = products[:, UNITS:] * scale
        hid_own[b] = (gated * jax.nn.sigmoid(gated) * lifted).astype(BF16)
        keep(hid_own.at[b], hid_all.at[b, n], f"HID{b}")
        def send_hid(k):
            put(hid_own.at[b], hid_all.at[b, n], f"HID{b}", c, z * NP + plane(k))
        loop(NP - 1, send_hid)

    arrived(wd.at[:, half], "WDF")
    for b in range(HB):
        arrived(hid_all.at[b], f"HID{b}")
        hidden = jnp.concatenate([hid_all[b, i] for i in range(NP)], axis=1)
        expert = jnp.dot(hidden, wd[...].reshape(NP * UNITS, COLS), preferred_element_type=F32)
        o_out[b] = (expert * gate_of[b]).astype(BF16).reshape(NZ, STRIP, COLS)
        keep(o_out.at[b, z], o_in.at[b, z], f"O{b}")
        def send_o(k):
            m = depth(k)
            put(o_out.at[b, m], o_in.at[b, z], f"O{b}", c, m * NP + n)
        loop(NZ - 1, send_o)

    for b in range(HB):
        arrived(o_in.at[b], f"O{b}")
        mixture = o_in[b, 0].astype(F32)
        for i in range(1, NZ):
            mixture = mixture + o_in[b, i].astype(F32)
        mix_out[2 * b:2 * b + 2] = mixture.reshape(2, OWN, COLS).astype(BF16)
        home(1, mix_out, mix_in, "MIX", 2 * b)
        home(1, mix_out, mix_in, "MIX", 2 * b + 1)

    def finish(landing, phase):
        arrived(landing, phase)
        for i in range(NP):
            out_ref[:, i * COLS:(i + 1) * COLS] = landing[i]

    @pl.when(c == 0)
    def _():
        finish(stream_in, "STREAM")

    @pl.when(c == 1)
    def _():
        finish(mix_in, "MIX")

    gone(qbuf, "Q")
    gone(resbuf, "RES")
    gone(selbuf, "SEL")
    gone(lat_in, "LATS")
    gone(wo.at[others, half], "WO")
    gone(wo.at[:, half], "WOF")
    gone(wgu.at[others, half_g, left], "WG")
    gone(wgu.at[:, half_g, left], "WGF")
    gone(wgu.at[others, half_g, right], "WU")
    gone(wgu.at[:, half_g, right], "WUF")
    gone(wd.at[others, half], "WD")
    gone(wd.at[:, half], "WDF")
    for b in range(HB):
        gone(head_all.at[b, others], f"HEAD{b}")
        gone(c_in.at[b, others], f"C{b}")
        gone(side_all.at[b, others], f"SIDE{b}")
        gone(sq_in.at[b, others], f"SQ{b}")
        gone(x_all.at[b, others], f"X{b}")
        gone(h_in.at[b, others], f"H{b}")
        gone(hid_all.at[b, others], f"HID{b}")
        gone(o_in.at[b, others], f"O{b}")

    def gone_home(core, src, phase):
        own = (c == core) & (xl == c)
        @pl.when(own)
        def _():
            gone(src.at[pl.ds(0, NY - 1)], phase)
        @pl.when(jnp.logical_not(own))
        def _():
            gone(src, phase)

    gone_home(0, stream_out, "STREAM")
    gone_home(1, mix_out, "MIX")


def per_device(
    queries, cache_pool, block_table, cache_len, w_uv, w_out, residual, norm_gain,
    expert_ids, expert_gates, w_gate, w_up, w_down,
):
    hbm = pl.BlockSpec(memory_space=pl.ANY)
    smem = pl.BlockSpec(memory_space=pltpu.SMEM)
    shapes = [
        ((KW, 512), BF16),
        ((64, OWN, KW), BF16),
        ((16, 64, KW), BF16),
        ((LAT, VH), BF16),
        ((1, COLS), F32),
        ((NH, OWN, KW), BF16),
        ((NH, OWN, LAT), BF16),
        ((HB, NZ, 2, OWN, LAT), BF16),
        ((OWN, 128), F32),
        ((NY, OWN, COLS), BF16),
        ((NY, OWN, 128), F32),
        ((NP, VH, COLS), BF16),
        ((NP, COLS, 2 * UNITS), BF16),
        ((NP, UNITS, COLS), BF16),
        ((HB, PART, VH), BF16),
        ((HB, NP, PART, VH), BF16),
        ((HB, NZ, STRIP, COLS), BF16),
        ((HB, NZ, STRIP, COLS), BF16),
        ((NY, OWN, COLS), BF16),
        ((NP, OWN, COLS), BF16),
        ((HB, NZ, STRIP, 128), F32),
        ((HB, 8, PART), F32),
        ((HB, NP, 8, PART), F32),
        ((HB, NZ, STRIP, COLS), BF16),
        ((HB, NP, PART, 2 * UNITS), BF16),
        ((HB, NP, PART, 2 * UNITS), BF16),
        ((HB, PART, UNITS), BF16),
        ((HB, NP, PART, UNITS), BF16),
        ((HB, NZ, STRIP, COLS), BF16),
        ((HB, NZ, STRIP, COLS), BF16),
        ((NY, OWN, COLS), BF16),
        ((NP, OWN, COLS), BF16),
    ]
    result = pl.pallas_call(
        kernel,
        out_shape=jax.ShapeDtypeStruct((OWN, D), BF16),
        in_specs=[hbm, hbm, smem, smem, hbm, hbm, hbm, hbm, smem, smem, hbm, hbm, hbm],
        out_specs=pl.BlockSpec(memory_space=pltpu.VMEM),
        scratch_shapes=[pltpu.VMEM(shape, dtype) for shape, dtype in shapes] + [
            pltpu.SemaphoreType.DMA((4,)),
            pltpu.SemaphoreType.DMA((len(NAMES),)),
            pltpu.SemaphoreType.DMA((len(NAMES),)),
        ],
        compiler_params=pltpu.CompilerParams(
            collective_id=0, has_side_effects=True, vmem_limit_bytes=60 * 1024 * 1024),
        cost_estimate=pl.CostEstimate(
            flops=4_000_000_000, bytes_accessed=16_000_000, transcendentals=400_000),
        name="layer",
    )(
        queries[0, :, 0, :].T, cache_pool[0], block_table[0].T, cache_len,
        w_uv[0], w_out[0], residual[0], norm_gain.reshape(1, D),
        expert_ids[0].T, expert_gates[0].T, w_gate[0], w_up[0], w_down[0],
    )
    return result[None, None]


def solution(mesh):
    in_specs = (
        P("sub", None, "head", None),
        P("sub", "head", None, None),
        P("sub", "head", None),
        P("sub", "head"),
        P("head", None, None),
        P("head", None, None),
        P("sub", "head", None),
        P(),
        P("sub", "head", None),
        P("sub", "head", None),
        P("head", None, None),
        P("head", None, None),
        P("head", None, None),
    )
    out_specs = P("side", "sub", "head", None)
    return jax.shard_map(
        per_device, mesh=mesh, in_specs=in_specs, out_specs=out_specs, check_vma=False
    )
```

```python
import jax
import jax.numpy as jnp
from jax import lax
from jax.experimental import pallas as pl
from jax.experimental.pallas import tpu as pltpu
from jax.sharding import PartitionSpec as P

D = 7168
LAT = 512
KW = 576
VH = 128
UNITS = 128
EPS = 1e-6
SCALE = 192 ** (-0.5)

NZ = 8
NP = 8
NY = 4
OWN = 8
COLS = D // NP
CHUNK = NY * OWN
ROWS = NZ * CHUNK
NH = NZ * NY
HB = 2
PART = ROWS // HB
STRIP = CHUNK // HB
MEET = 2 * NH + 2 * NP - 1 + NZ - 1
F32 = jnp.float32
BF16 = jnp.bfloat16


NAMES = (
    ["Q0", "Q1", "RES", "SEL", "LATS", "STREAM", "MIX"]
    + [name + step for name in ("WO", "WG", "WU", "WD") for step in ("", "F")]
    + [name + str(b) for name in ("HEAD", "C", "SIDE", "SQ", "X", "H", "HID", "O") for b in range(HB)]
)
NEAR = 5
SPANS = ((0, NEAR), (NEAR, NZ))
PHASE = {name: i for i, name in enumerate(NAMES)}


def kernel(
    q_ref, pool_ref, tab_ref, len_ref, wuv_ref, wout_ref, res_ref, gain_ref,
    ids_ref, gates_ref, wg_ref, wu_ref, wd_ref,
    out_ref,
    qcols, qrows, pool, wuv, gain, qbuf, lat_out, lat_in, sel, resbuf, selbuf,
    wo, wgu, wd, head_own, head_all, c_out, c_in,
    stream_out, stream_in, side_all, sq_own, sq_in, x_all,
    h_out, h_in, hid_own, hid_all, o_out, o_in, mix_out, mix_in,
    load, send, recv,
):
    c = lax.axis_index("side")
    h = lax.axis_index("head")
    sub = lax.axis_index("sub")
    z, n = h // NP, h % NP
    xl, y = n // NY, n % NY
    spot = z * NY + y

    def device(core, head):
        return (core, head, sub)

    def put(src, dst, phase, core, head):
        pltpu.make_async_remote_copy(
            src_ref=src, dst_ref=dst,
            send_sem=send.at[PHASE[phase]], recv_sem=recv.at[PHASE[phase]],
            device_id=device(core, head), device_id_type=pl.DeviceIdType.MESH,
        ).start()

    def keep(src, dst, phase):
        pltpu.make_async_copy(src, dst, recv.at[PHASE[phase]]).start()

    def arrived(ref, phase):
        with jax.named_scope("w_" + phase):
            pltpu.make_async_copy(ref, ref, recv.at[PHASE[phase]]).wait()

    def gone(ref, phase):
        pltpu.make_async_copy(ref, ref, send.at[PHASE[phase]]).wait()

    def loop(count, body):
        def step(k, carry):
            body(k)
            return carry
        lax.fori_loop(0, count, step, 0)

    def around(k, me, size):
        far = (k + 1) // 2
        return (me + size + far * (2 * (k % 2) - 1)) % size

    def depth(k):
        return around(k + 1, z, NZ)

    def plane(k):
        turn = jnp.where(k < 4, 1 + 2 * (k % 2), jnp.where(k == 4, 0, 2))
        flip = jnp.where(k < 4, k // 2, jnp.where(k == 5, 0, 1))
        return ((xl + flip) % 2) * NY + (y + turn) % NY

    def cols(m):
        return pl.ds(pl.multiple_of(m * COLS, 128), COLS)

    loads = [
        pltpu.make_async_copy(q_ref, qcols, load.at[0]),
        pltpu.make_async_copy(pool_ref, pool, load.at[1]),
        pltpu.make_async_copy(wuv_ref, wuv, load.at[2]),
        pltpu.make_async_copy(gain_ref.at[:, cols(n)], gain, load.at[3]),
    ]
    for copy in loads:
        copy.start()

    barrier = pltpu.get_barrier_semaphore()

    def greet(core, head):
        pl.semaphore_signal(
            barrier, inc=1, device_id=device(core, head), device_id_type=pl.DeviceIdType.MESH)

    def greet_far(k):
        m = around(k, spot, NH)
        greet(1 - xl, (m // NY) * NP + c * NY + m % NY)
        greet(xl, (m // NY) * NP + (1 - c) * NY + m % NY)
    loop(NH, greet_far)

    def greet_plane(k):
        m = (c * NP + n + k + 1) % (2 * NP)
        greet(m // NP, z * NP + m % NP)
    loop(2 * NP - 1, greet_plane)

    def greet_depth(k):
        greet(c, depth(k) * NP + n)
    loop(NZ - 1, greet_depth)

    loads[0].wait()
    for i in range(0, KW, 128):
        wide = min(128, KW - i)
        turned = jnp.transpose(qcols[i:i + wide, :].astype(F32))
        qrows[:, :, i:i + wide] = turned.reshape(64, OWN, wide).astype(BF16)

    with jax.named_scope("w_barrier"):
        pl.semaphore_wait(barrier, MEET)

    for a, (first, last) in enumerate(SPANS):
        def send_query(k):
            p = first + k // NY
            level = (z + NZ - around(p, 0, NZ)) % NZ
            owner = level * NP + c * NY + (y + k) % NY
            put(qrows.at[owner], qbuf.at[p * NY + y], f"Q{a}", 1 - xl, owner)
        loop((last - first) * NY, send_query)

    lane = lax.broadcasted_iota(jnp.int32, (OWN, 128), 1)
    line = lax.broadcasted_iota(jnp.int32, (OWN, 128), 0)
    picked = jnp.zeros((OWN, 128), F32)
    for r in range(OWN):
        for k in range(ids_ref.shape[0]):
            picked = picked + jnp.where((line == r) & (lane == ids_ref[k, r]), gates_ref[k, r], 0.0)
    sel[...] = picked

    def send_residual(k):
        m = (1 - c) * NY + (y + k) % NY
        put(res_ref.at[:, cols(m)], resbuf.at[y], "RES", xl, z * NP + m)
        put(sel, selbuf.at[y], "SEL", xl, z * NP + m)
    loop(NY, send_residual)

    left, right = pl.ds(0, UNITS), pl.ds(UNITS, UNITS)
    arrays = {
        "WO": (VH, lambda m, i, r: wout_ref.at[r, cols(m)], lambda i, r: wo.at[i, r]),
        "WG": (COLS, lambda m, i, r: wg_ref.at[i], lambda i, r: wgu.at[i, r, left]),
        "WU": (COLS, lambda m, i, r: wu_ref.at[i], lambda i, r: wgu.at[i, r, right]),
        "WD": (UNITS, lambda m, i, r: wd_ref.at[r, cols(m)], lambda i, r: wd.at[i, r]),
    }
    every, others = pl.ds(0, NP), pl.ds(0, NP - 1)

    def halves(name):
        size = arrays[name][0] // 2
        return pl.ds(pl.multiple_of(c * size, size), size)

    def share(name, first=0, last=NP - 1):
        depth_of, source, landing = arrays[name]
        rows = halves(name)
        size = rows.size
        place = landing(n, rows)
        def take(m):
            deep = pl.ds(pl.multiple_of(m * depth_of + rows.start, size), size)
            return source(m, deep, rows)
        if first == 0:
            keep(take(n), place, name)
        def step(k):
            m = plane(k + first)
            put(take(m), place, name, c, z * NP + m)
        loop(last - first, step)

    def pass_on(name):
        mine = arrays[name][2](every, halves(name))
        arrived(mine, name)
        put(mine, mine, name + "F", 1 - c, h)

    def ready(name):
        arrived(arrays[name][2](every, halves(name)), name + "F")

    share("WO")
    row = lax.broadcasted_iota(jnp.int32, (OWN, 1024), 0)
    place = lax.broadcasted_iota(jnp.int32, (OWN, 1024), 1)
    block, offset = place // 64, place % 64
    bias = jnp.full((OWN, 1024), -1e30, F32)
    for r in range(OWN):
        seen = ((block == tab_ref[0, r]) & (offset < len_ref[0, r])) | (
            (block == tab_ref[1, r]) & (offset + 64 < len_ref[0, r]))
        bias = jnp.where((row == r) & seen, 0.0, bias)


    loads[1].wait()
    keys = pool[...].reshape(1024, KW)
    values = keys[:, :LAT]
    for a, (first, last) in enumerate(SPANS):
        heads_at_once = (last - first) * NY
        some = slice(first * NY, last * NY)
        arrived(qbuf.at[some], f"Q{a}")
        queries = qbuf[some].astype(F32).reshape(heads_at_once * OWN, KW).astype(BF16)
        scores = lax.dot_general(
            queries, keys, (((1,), (1,)), ((), ())), preferred_element_type=F32)
        scores = scores.reshape(heads_at_once, OWN, 1024) * SCALE + bias[None]
        scores = scores.reshape(heads_at_once * OWN, 1024)
        peak = jnp.max(scores, axis=-1, keepdims=True)
        raw = jnp.exp(scores - peak)
        total = jnp.sum(raw, axis=-1, keepdims=True)
        high = raw.astype(BF16)
        low = (raw - high.astype(F32)).astype(BF16)
        latents = jnp.dot(high, values, preferred_element_type=F32)
        latents = (latents + jnp.dot(low, values, preferred_element_type=F32)) / total
        lat_out[some] = latents.reshape(heads_at_once, OWN, LAT).astype(BF16)

        def send_latent(k):
            p, m = first + k // NY, (y + k) % NY
            head = (z + around(p, 0, NZ)) % NZ * NP + (1 - c) * NY + m
            put(lat_out.at[p * NY + m], lat_in.at[y // 2, z, y % 2], "LATS", xl, head)
        loop(heads_at_once, send_latent)

    share("WG", 0, 4)


    loads[2].wait()
    arrived(lat_in, "LATS")
    for b in range(HB):
        rows = lat_in[b].astype(F32).reshape(PART, LAT).astype(BF16)
        head_own[b] = jnp.dot(rows, wuv[...], preferred_element_type=F32).astype(BF16)
        keep(head_own.at[b], head_all.at[b, n], f"HEAD{b}")
        def send_head(k):
            put(head_own.at[b], head_all.at[b, n], f"HEAD{b}", c, z * NP + plane(k))
        loop(NP - 1, send_head)

    pass_on("WO")
    share("WG", 4)
    share("WU")
    ready("WO")
    for b in range(HB):
        arrived(head_all.at[b], f"HEAD{b}")
        heads = jnp.concatenate([head_all[b, i] for i in range(NP)], axis=1)
        partial = jnp.dot(heads, wo[...].reshape(NP * VH, COLS), preferred_element_type=F32)
        c_out[b] = partial.astype(BF16).reshape(NZ, STRIP, COLS)
        keep(c_out.at[b, z], c_in.at[b, z], f"C{b}")
        def send_c(k):
            m = depth(k)
            put(c_out.at[b, m], c_in.at[b, z], f"C{b}", c, m * NP + n)
        loop(NZ - 1, send_c)

    share("WD")

    def home(core, src, landing, phase, k):
        own = (c == core) & (xl == c) & (y == k)
        @pl.when(own)
        def _():
            keep(src.at[k], landing.at[n], phase)
        @pl.when(jnp.logical_not(own))
        def _():
            put(src.at[k], landing.at[n], phase, core, z * NP + c * NY + k)

    arrived(resbuf, "RES")
    arrived(selbuf, "SEL")
    loads[3].wait()
    for b in range(HB):
        pair = slice(2 * b, 2 * b + 2)
        arrived(c_in.at[b], f"C{b}")
        attended = c_in[b, 0].astype(F32)
        for i in range(1, NZ):
            attended = attended + c_in[b, i].astype(F32)
        residual = resbuf[pair].astype(F32).reshape(STRIP, COLS)
        stream = (residual + attended).astype(BF16).astype(F32)
        x_all[b, z] = (stream * gain[...]).astype(BF16)
        def send_x(k):
            put(x_all.at[b, z], x_all.at[b, z], f"X{b}", c, depth(k) * NP + n)
        loop(NZ - 1, send_x)

        squares = jnp.sum(stream * stream, axis=-1, keepdims=True)
        wide = lax.broadcasted_iota(jnp.int32, (STRIP, 128), 1)
        chosen = selbuf[pair].reshape(STRIP, 128)
        side_all[b, z] = jnp.where(wide < 8, chosen, squares)
        def send_side(k):
            put(side_all.at[b, z], side_all.at[b, z], f"SIDE{b}", c, depth(k) * NP + n)
        loop(NZ - 1, send_side)

        stream_out[pair] = stream.reshape(2, OWN, COLS).astype(BF16)
        home(0, stream_out, stream_in, "STREAM", 2 * b)
        home(0, stream_out, stream_in, "STREAM", 2 * b + 1)

    pass_on("WG")
    pass_on("WU")

    ready("WG")
    ready("WU")
    lanes = lax.broadcasted_iota(jnp.int32, (PART, 128), 1)
    gate_of = []

    def begin(b):
        arrived(side_all.at[b, others], f"SIDE{b}")
        tiles = side_all[b].reshape(PART, 128)
        gate_of.append(jnp.sum(jnp.where(lanes == z, tiles, 0.0), axis=-1, keepdims=True))
        sq_own[b] = jnp.transpose(tiles)[8:16]
        keep(sq_own.at[b], sq_in.at[b, n], f"SQ{b}")
        def send_sq(k):
            put(sq_own.at[b], sq_in.at[b, n], f"SQ{b}", c, z * NP + plane(k))
        loop(NP - 1, send_sq)
        arrived(x_all.at[b, others], f"X{b}")

    def lift(b, first, last):
        x = x_all[b].reshape(PART, COLS)
        def send_h(k):
            m = plane(k + first)
            h_out[b, m] = jnp.dot(x, wgu[m], preferred_element_type=F32).astype(BF16)
            put(h_out.at[b, m], h_in.at[b, n], f"H{b}", c, z * NP + m)
        loop(last - first, send_h)
        if last == NP - 1:
            h_out[b, n] = jnp.dot(x, wgu[n], preferred_element_type=F32).astype(BF16)
            keep(h_out.at[b, n], h_in.at[b, n], f"H{b}")

    def join(b):
        arrived(sq_in.at[b], f"SQ{b}")
        square = sq_in[b, 0]
        for i in range(1, NP):
            square = square + sq_in[b, i]
        scale = lax.rsqrt(square * (1.0 / D) + EPS)
        scale = jnp.transpose(jnp.broadcast_to(scale[0:1], (128, PART)))

        arrived(h_in.at[b], f"H{b}")
        products = h_in[b, 0].astype(F32)
        for i in range(1, NP):
            products = products + h_in[b, i].astype(F32)
        gated = products[:, :UNITS] * scale
        lifted = products[:, UNITS:] * scale
        hid_own[b] = (gated * jax.nn.sigmoid(gated) * lifted).astype(BF16)
        keep(hid_own.at[b], hid_all.at[b, n], f"HID{b}")
        def send_hid(k):
            put(hid_own.at[b], hid_all.at[b, n], f"HID{b}", c, z * NP + plane(k))
        loop(NP - 1, send_hid)

    begin(0)
    lift(0, 0, NP - 1)
    begin(1)
    lift(1, 0, NP - 1)
    pass_on("WD")
    join(0)
    join(1)

    ready("WD")
    for b in range(HB):
        arrived(hid_all.at[b], f"HID{b}")
        hidden = jnp.concatenate([hid_all[b, i] for i in range(NP)], axis=1)
        expert = jnp.dot(hidden, wd[...].reshape(NP * UNITS, COLS), preferred_element_type=F32)
        o_out[b] = (expert * gate_of[b]).astype(BF16).reshape(NZ, STRIP, COLS)
        keep(o_out.at[b, z], o_in.at[b, z], f"O{b}")
        def send_o(k):
            m = depth(k)
            put(o_out.at[b, m], o_in.at[b, z], f"O{b}", c, m * NP + n)
        loop(NZ - 1, send_o)

    for b in range(HB):
        arrived(o_in.at[b], f"O{b}")
        mixture = o_in[b, 0].astype(F32)
        for i in range(1, NZ):
            mixture = mixture + o_in[b, i].astype(F32)
        mix_out[2 * b:2 * b + 2] = mixture.reshape(2, OWN, COLS).astype(BF16)
        home(1, mix_out, mix_in, "MIX", 2 * b)
        home(1, mix_out, mix_in, "MIX", 2 * b + 1)

    def finish(landing, phase):
        arrived(landing, phase)
        for i in range(NP):
            out_ref[:, i * COLS:(i + 1) * COLS] = landing[i]

    @pl.when(c == 0)
    def _():
        finish(stream_in, "STREAM")

    @pl.when(c == 1)
    def _():
        finish(mix_in, "MIX")

    for a, (first, last) in enumerate(SPANS):
        gone(qbuf.at[first * NY:last * NY], f"Q{a}")
    gone(resbuf, "RES")
    gone(selbuf, "SEL")
    gone(lat_in, "LATS")
    for name, (_, _, landing) in arrays.items():
        gone(landing(others, halves(name)), name)
        gone(landing(every, halves(name)), name + "F")
    for b in range(HB):
        gone(head_all.at[b, others], f"HEAD{b}")
        gone(c_in.at[b, others], f"C{b}")
        gone(side_all.at[b, others], f"SIDE{b}")
        gone(sq_in.at[b, others], f"SQ{b}")
        gone(x_all.at[b, others], f"X{b}")
        gone(h_in.at[b, others], f"H{b}")
        gone(hid_all.at[b, others], f"HID{b}")
        gone(o_in.at[b, others], f"O{b}")

    def gone_home(core, src, phase):
        own = (c == core) & (xl == c)
        @pl.when(own)
        def _():
            gone(src.at[pl.ds(0, NY - 1)], phase)
        @pl.when(jnp.logical_not(own))
        def _():
            gone(src, phase)

    gone_home(0, stream_out, "STREAM")
    gone_home(1, mix_out, "MIX")


def per_device(
    queries, cache_pool, block_table, cache_len, w_uv, w_out, residual, norm_gain,
    expert_ids, expert_gates, w_gate, w_up, w_down,
):
    hbm = pl.BlockSpec(memory_space=pl.ANY)
    smem = pl.BlockSpec(memory_space=pltpu.SMEM)
    shapes = [
        ((KW, 512), BF16),
        ((64, OWN, KW), BF16),
        ((16, 64, KW), BF16),
        ((LAT, VH), BF16),
        ((1, COLS), F32),
        ((NH, OWN, KW), BF16),
        ((NH, OWN, LAT), BF16),
        ((HB, NZ, 2, OWN, LAT), BF16),
        ((OWN, 128), F32),
        ((NY, OWN, COLS), BF16),
        ((NY, OWN, 128), F32),
        ((NP, VH, COLS), BF16),
        ((NP, COLS, 2 * UNITS), BF16),
        ((NP, UNITS, COLS), BF16),
        ((HB, PART, VH), BF16),
        ((HB, NP, PART, VH), BF16),
        ((HB, NZ, STRIP, COLS), BF16),
        ((HB, NZ, STRIP, COLS), BF16),
        ((NY, OWN, COLS), BF16),
        ((NP, OWN, COLS), BF16),
        ((HB, NZ, STRIP, 128), F32),
        ((HB, 8, PART), F32),
        ((HB, NP, 8, PART), F32),
        ((HB, NZ, STRIP, COLS), BF16),
        ((HB, NP, PART, 2 * UNITS), BF16),
        ((HB, NP, PART, 2 * UNITS), BF16),
        ((HB, PART, UNITS), BF16),
        ((HB, NP, PART, UNITS), BF16),
        ((HB, NZ, STRIP, COLS), BF16),
        ((HB, NZ, STRIP, COLS), BF16),
        ((NY, OWN, COLS), BF16),
        ((NP, OWN, COLS), BF16),
    ]
    result = pl.pallas_call(
        kernel,
        out_shape=jax.ShapeDtypeStruct((OWN, D), BF16),
        in_specs=[hbm, hbm, smem, smem, hbm, hbm, hbm, hbm, smem, smem, hbm, hbm, hbm],
        out_specs=pl.BlockSpec(memory_space=pltpu.VMEM),
        scratch_shapes=[pltpu.VMEM(shape, dtype) for shape, dtype in shapes] + [
            pltpu.SemaphoreType.DMA((4,)),
            pltpu.SemaphoreType.DMA((len(NAMES),)),
            pltpu.SemaphoreType.DMA((len(NAMES),)),
        ],
        compiler_params=pltpu.CompilerParams(
            collective_id=0, has_side_effects=True, vmem_limit_bytes=60 * 1024 * 1024),
        cost_estimate=pl.CostEstimate(
            flops=4_000_000_000, bytes_accessed=16_000_000, transcendentals=400_000),
        name="layer",
    )(
        queries[0, :, 0, :].T, cache_pool[0], block_table[0].T, cache_len,
        w_uv[0], w_out[0], residual[0], norm_gain.reshape(1, D),
        expert_ids[0].T, expert_gates[0].T, w_gate[0], w_up[0], w_down[0],
    )
    return result[None, None]


def solution(mesh):
    in_specs = (
        P("sub", None, "head", None),
        P("sub", "head", None, None),
        P("sub", "head", None),
        P("sub", "head"),
        P("head", None, None),
        P("head", None, None),
        P("sub", "head", None),
        P(),
        P("sub", "head", None),
        P("sub", "head", None),
        P("head", None, None),
        P("head", None, None),
        P("head", None, None),
    )
    out_specs = P("side", "sub", "head", None)
    return jax.shard_map(
        per_device, mesh=mesh, in_specs=in_specs, out_specs=out_specs, check_vma=False
    )
```

```python
import jax
import jax.numpy as jnp
from jax import lax
from jax.experimental import pallas as pl
from jax.experimental.pallas import tpu as pltpu
from jax.sharding import PartitionSpec as P

D = 7168
LAT = 512
KW = 576
VH = 128
UNITS = 128
EPS = 1e-6
SCALE = 192 ** (-0.5)

NZ = 8
NP = 8
NY = 4
OWN = 8
COLS = D // NP
CHUNK = NY * OWN
ROWS = NZ * CHUNK
NH = NZ * NY
HB = 2
PART = ROWS // HB
STRIP = CHUNK // HB
MEET = 2 * NH + 2 * NP - 1 + NZ - 1
F32 = jnp.float32
BF16 = jnp.bfloat16


NAMES = (
    ["Q0", "Q1", "RES", "SEL", "LATS", "STREAM", "MIX"]
    + [name + step for name in ("WO", "WG", "WU", "WD") for step in ("", "F")]
    + [name + str(b) for name in ("HEAD", "C", "SIDE", "SQ", "X", "H", "HID", "O") for b in range(HB)]
)
NEAR = 5
SPANS = ((0, NEAR), (NEAR, NZ))
PHASE = {name: i for i, name in enumerate(NAMES)}


def kernel(
    q_ref, pool_ref, tab_ref, len_ref, wuv_ref, wout_ref, res_ref, gain_ref,
    ids_ref, gates_ref, wg_ref, wu_ref, wd_ref,
    out_ref,
    qcols, qrows, pool, wuv, gain, qbuf, lat_out, lat_in, sel, resbuf, selbuf,
    wo, wgu, wd, head_own, head_all, c_out, c_in,
    stream_out, side_all, sq_own, sq_in, x_all,
    h_out, h_in, hid_own, hid_all, o_out, o_in, mix_out,
    load, send, recv,
):
    c = lax.axis_index("side")
    h = lax.axis_index("head")
    sub = lax.axis_index("sub")
    z, n = h // NP, h % NP
    xl, y = n // NY, n % NY
    spot = z * NY + y

    def device(core, head):
        return (core, head, sub)

    def put(src, dst, phase, core, head):
        pltpu.make_async_remote_copy(
            src_ref=src, dst_ref=dst,
            send_sem=send.at[PHASE[phase]], recv_sem=recv.at[PHASE[phase]],
            device_id=device(core, head), device_id_type=pl.DeviceIdType.MESH,
        ).start()

    def keep(src, dst, phase):
        pltpu.make_async_copy(src, dst, recv.at[PHASE[phase]]).start()

    def arrived(ref, phase):
        with jax.named_scope("w_" + phase):
            pltpu.make_async_copy(ref, ref, recv.at[PHASE[phase]]).wait()

    def gone(ref, phase):
        pltpu.make_async_copy(ref, ref, send.at[PHASE[phase]]).wait()

    def loop(count, body):
        def step(k, carry):
            body(k)
            return carry
        lax.fori_loop(0, count, step, 0)

    def around(k, me, size):
        far = (k + 1) // 2
        return (me + size + far * (2 * (k % 2) - 1)) % size

    def depth(k):
        return around(NZ - 1 - k, z, NZ)

    def plane(k):
        turn = jnp.where(k < 2, 2, jnp.where(k < 6, 1 + 2 * (k % 2), 0))
        flip = jnp.where(k < 2, k, jnp.where(k < 4, 0, 1))
        return ((xl + flip) % 2) * NY + (y + turn) % NY

    def cols(m):
        return pl.ds(pl.multiple_of(m * COLS, 128), COLS)

    loads = [
        pltpu.make_async_copy(q_ref, qcols, load.at[0]),
        pltpu.make_async_copy(pool_ref, pool, load.at[1]),
        pltpu.make_async_copy(wuv_ref, wuv, load.at[2]),
        pltpu.make_async_copy(gain_ref.at[:, cols(n)], gain, load.at[3]),
    ]
    for copy in loads:
        copy.start()

    barrier = pltpu.get_barrier_semaphore()

    def greet(core, head):
        pl.semaphore_signal(
            barrier, inc=1, device_id=device(core, head), device_id_type=pl.DeviceIdType.MESH)

    def greet_far(level):
        for m in range(NY):
            greet(1 - xl, level * NP + c * NY + m)
            greet(xl, level * NP + (1 - c) * NY + m)
    loop(NZ, greet_far)

    def greet_plane(k):
        m = (c * NP + n + k + 1) % (2 * NP)
        greet(m // NP, z * NP + m % NP)
    loop(2 * NP - 1, greet_plane)

    def greet_depth(k):
        greet(c, depth(k) * NP + n)
    loop(NZ - 1, greet_depth)

    loads[0].wait()
    for i in range(0, KW, 128):
        wide = min(128, KW - i)
        turned = jnp.transpose(qcols[i:i + wide, :].astype(F32))
        qrows[:, :, i:i + wide] = turned.reshape(64, OWN, wide).astype(BF16)

    with jax.named_scope("w_barrier"):
        pl.semaphore_wait(barrier, MEET)

    for a, (first, last) in enumerate(SPANS):
        def send_query(k):
            p = first + k // NY
            level = (z + NZ - around(p, 0, NZ)) % NZ
            owner = level * NP + c * NY + (y + k) % NY
            put(qrows.at[owner], qbuf.at[p * NY + y], f"Q{a}", 1 - xl, owner)
        loop((last - first) * NY, send_query)

    lane = lax.broadcasted_iota(jnp.int32, (OWN, 128), 1)
    line = lax.broadcasted_iota(jnp.int32, (OWN, 128), 0)
    picked = jnp.zeros((OWN, 128), F32)
    for r in range(OWN):
        for k in range(ids_ref.shape[0]):
            picked = picked + jnp.where((line == r) & (lane == ids_ref[k, r]), gates_ref[k, r], 0.0)
    sel[...] = picked

    def send_residual(k):
        m = (1 - c) * NY + (y + k) % NY
        put(res_ref.at[:, cols(m)], resbuf.at[y], "RES", xl, z * NP + m)
        put(sel, selbuf.at[y], "SEL", xl, z * NP + m)
    loop(NY, send_residual)

    left, right = pl.ds(0, UNITS), pl.ds(UNITS, UNITS)
    arrays = {
        "WO": (VH, lambda m, i, r: wout_ref.at[r, cols(m)], lambda i, r: wo.at[i, r]),
        "WG": (COLS, lambda m, i, r: wg_ref.at[i], lambda i, r: wgu.at[i, r, left]),
        "WU": (COLS, lambda m, i, r: wu_ref.at[i], lambda i, r: wgu.at[i, r, right]),
        "WD": (UNITS, lambda m, i, r: wd_ref.at[r, cols(m)], lambda i, r: wd.at[i, r]),
    }
    every, others = pl.ds(0, NP), pl.ds(0, NP - 1)

    def halves(name):
        size = arrays[name][0] // 2
        return pl.ds(pl.multiple_of(c * size, size), size)

    def share(name, first=0, last=NP - 1):
        depth_of, source, landing = arrays[name]
        rows = halves(name)
        size = rows.size
        place = landing(n, rows)
        def take(m):
            deep = pl.ds(pl.multiple_of(m * depth_of + rows.start, size), size)
            return source(m, deep, rows)
        if last == NP - 1:
            keep(take(n), place, name)
        def step(k):
            m = plane(k + first)
            put(take(m), place, name, c, z * NP + m)
        loop(last - first, step)

    def pass_on(name):
        mine = arrays[name][2](every, halves(name))
        arrived(mine, name)
        put(mine, mine, name + "F", 1 - c, h)

    def ready(name):
        arrived(arrays[name][2](every, halves(name)), name + "F")

    share("WO")
    row = lax.broadcasted_iota(jnp.int32, (OWN, 1024), 0)
    place = lax.broadcasted_iota(jnp.int32, (OWN, 1024), 1)
    block, offset = place // 64, place % 64
    bias = jnp.full((OWN, 1024), -1e30, F32)
    for r in range(OWN):
        seen = ((block == tab_ref[0, r]) & (offset < len_ref[0, r])) | (
            (block == tab_ref[1, r]) & (offset + 64 < len_ref[0, r]))
        bias = jnp.where((row == r) & seen, 0.0, bias)


    loads[1].wait()
    keys = pool[...].reshape(1024, KW)
    values = keys[:, :LAT]
    for a, (first, last) in enumerate(SPANS):
        heads_at_once = (last - first) * NY
        some = slice(first * NY, last * NY)
        arrived(qbuf.at[some], f"Q{a}")
        queries = qbuf[some].astype(F32).reshape(heads_at_once * OWN, KW).astype(BF16)
        scores = lax.dot_general(
            queries, keys, (((1,), (1,)), ((), ())), preferred_element_type=F32)
        scores = scores.reshape(heads_at_once, OWN, 1024) * SCALE + bias[None]
        scores = scores.reshape(heads_at_once * OWN, 1024)
        peak = jnp.max(scores, axis=-1, keepdims=True)
        raw = jnp.exp(scores - peak)
        total = jnp.sum(raw, axis=-1, keepdims=True)
        high = raw.astype(BF16)
        low = (raw - high.astype(F32)).astype(BF16)
        latents = jnp.dot(high, values, preferred_element_type=F32)
        latents = (latents + jnp.dot(low, values, preferred_element_type=F32)) / total
        lat_out[some] = latents.reshape(heads_at_once, OWN, LAT).astype(BF16)

        def send_latent(k):
            p, m = first + k // NY, (y + k) % NY
            head = (z + around(p, 0, NZ)) % NZ * NP + (1 - c) * NY + m
            put(lat_out.at[p * NY + m], lat_in.at[y // 2, z, y % 2], "LATS", xl, head)
        loop(heads_at_once, send_latent)

    share("WG", 2)


    loads[2].wait()
    arrived(lat_in, "LATS")
    for b in range(HB):
        rows = lat_in[b].astype(F32).reshape(PART, LAT).astype(BF16)
        head_own[b] = jnp.dot(rows, wuv[...], preferred_element_type=F32).astype(BF16)
        keep(head_own.at[b], head_all.at[b, n], f"HEAD{b}")
        def send_head(k):
            put(head_own.at[b], head_all.at[b, n], f"HEAD{b}", c, z * NP + plane(k))
        loop(NP - 1, send_head)

    pass_on("WO")
    share("WG", 0, 2)
    share("WU")
    ready("WO")
    for b in range(HB):
        arrived(head_all.at[b], f"HEAD{b}")
        heads = jnp.concatenate([head_all[b, i] for i in range(NP)], axis=1)
        partial = jnp.dot(heads, wo[...].reshape(NP * VH, COLS), preferred_element_type=F32)
        c_out[b] = partial.astype(BF16).reshape(NZ, STRIP, COLS)
        keep(c_out.at[b, z], c_in.at[b, z], f"C{b}")
        def send_c(k):
            m = depth(k)
            put(c_out.at[b, m], c_in.at[b, z], f"C{b}", c, m * NP + n)
        loop(NZ - 1, send_c)

    share("WD")

    def home(core, src, landing, phase, k):
        own = (c == core) & (xl == c) & (y == k)
        @pl.when(own)
        def _():
            keep(src.at[k], landing.at[n], phase)
        @pl.when(jnp.logical_not(own))
        def _():
            put(src.at[k], landing.at[n], phase, core, z * NP + c * NY + k)

    arrived(resbuf, "RES")
    arrived(selbuf, "SEL")
    loads[3].wait()
    for b in range(HB):
        pair = slice(2 * b, 2 * b + 2)
        arrived(c_in.at[b], f"C{b}")
        attended = c_in[b, 0].astype(F32)
        for i in range(1, NZ):
            attended = attended + c_in[b, i].astype(F32)
        residual = resbuf[pair].astype(F32).reshape(STRIP, COLS)
        stream = (residual + attended).astype(BF16).astype(F32)
        x_all[b, z] = (stream * gain[...]).astype(BF16)
        def send_x(k):
            put(x_all.at[b, z], x_all.at[b, z], f"X{b}", c, depth(k) * NP + n)
        loop(NZ - 1, send_x)

        squares = jnp.sum(stream * stream, axis=-1, keepdims=True)
        wide = lax.broadcasted_iota(jnp.int32, (STRIP, 128), 1)
        chosen = selbuf[pair].reshape(STRIP, 128)
        side_all[b, z] = jnp.where(wide < 8, chosen, squares)
        def send_side(k):
            put(side_all.at[b, z], side_all.at[b, z], f"SIDE{b}", c, depth(k) * NP + n)
        loop(NZ - 1, send_side)

        stream_out[pair] = stream.reshape(2, OWN, COLS).astype(BF16)
        home(0, stream_out, out_ref, "STREAM", 2 * b)
        home(0, stream_out, out_ref, "STREAM", 2 * b + 1)

    pass_on("WG")
    pass_on("WU")

    ready("WG")
    ready("WU")
    lanes = lax.broadcasted_iota(jnp.int32, (PART, 128), 1)
    gate_of = []

    def begin(b):
        arrived(side_all.at[b, others], f"SIDE{b}")
        tiles = side_all[b].reshape(PART, 128)
        gate_of.append(jnp.sum(jnp.where(lanes == z, tiles, 0.0), axis=-1, keepdims=True))
        sq_own[b] = jnp.transpose(tiles)[8:16]
        keep(sq_own.at[b], sq_in.at[b, n], f"SQ{b}")
        def send_sq(k):
            put(sq_own.at[b], sq_in.at[b, n], f"SQ{b}", c, z * NP + plane(k))
        loop(NP - 1, send_sq)

    def lift(b, first, last):
        arrived(x_all.at[b, others], f"X{b}")
        x = x_all[b].reshape(PART, COLS)
        def send_h(k):
            m = plane(k + first)
            h_out[b, m] = jnp.dot(x, wgu[m], preferred_element_type=F32).astype(BF16)
            put(h_out.at[b, m], h_in.at[b, n], f"H{b}", c, z * NP + m)
        loop(last - first, send_h)
        if last == NP - 1:
            h_out[b, n] = jnp.dot(x, wgu[n], preferred_element_type=F32).astype(BF16)
            keep(h_out.at[b, n], h_in.at[b, n], f"H{b}")

    def join(b):
        arrived(sq_in.at[b], f"SQ{b}")
        square = sq_in[b, 0]
        for i in range(1, NP):
            square = square + sq_in[b, i]
        scale = lax.rsqrt(square * (1.0 / D) + EPS)
        scale = jnp.transpose(jnp.broadcast_to(scale[0:1], (128, PART)))

        arrived(h_in.at[b], f"H{b}")
        products = h_in[b, 0].astype(F32)
        for i in range(1, NP):
            products = products + h_in[b, i].astype(F32)
        gated = products[:, :UNITS] * scale
        lifted = products[:, UNITS:] * scale
        hid_own[b] = (gated * jax.nn.sigmoid(gated) * lifted).astype(BF16)
        keep(hid_own.at[b], hid_all.at[b, n], f"HID{b}")
        def send_hid(k):
            put(hid_own.at[b], hid_all.at[b, n], f"HID{b}", c, z * NP + plane(k))
        loop(NP - 1, send_hid)

    lift(0, 0, NP - 1)
    begin(0)
    lift(1, 0, NP - 1)
    begin(1)
    pass_on("WD")
    join(0)
    join(1)

    ready("WD")
    for b in range(HB):
        arrived(hid_all.at[b], f"HID{b}")
        hidden = jnp.concatenate([hid_all[b, i] for i in range(NP)], axis=1)
        expert = jnp.dot(hidden, wd[...].reshape(NP * UNITS, COLS), preferred_element_type=F32)
        o_out[b] = (expert * gate_of[b]).astype(BF16).reshape(NZ, STRIP, COLS)
        keep(o_out.at[b, z], o_in.at[b, z], f"O{b}")
        def send_o(k):
            m = depth(k)
            put(o_out.at[b, m], o_in.at[b, z], f"O{b}", c, m * NP + n)
        loop(NZ - 1, send_o)

    for b in range(HB):
        arrived(o_in.at[b], f"O{b}")
        mixture = o_in[b, 0].astype(F32)
        for i in range(1, NZ):
            mixture = mixture + o_in[b, i].astype(F32)
        mix_out[2 * b:2 * b + 2] = mixture.reshape(2, OWN, COLS).astype(BF16)
        home(1, mix_out, out_ref, "MIX", 2 * b)
        home(1, mix_out, out_ref, "MIX", 2 * b + 1)

    for a, (first, last) in enumerate(SPANS):
        gone(qbuf.at[first * NY:last * NY], f"Q{a}")
    gone(resbuf, "RES")
    gone(selbuf, "SEL")
    gone(lat_in, "LATS")
    for name, (_, _, landing) in arrays.items():
        gone(landing(others, halves(name)), name)
        gone(landing(every, halves(name)), name + "F")
    for b in range(HB):
        gone(head_all.at[b, others], f"HEAD{b}")
        gone(c_in.at[b, others], f"C{b}")
        gone(side_all.at[b, others], f"SIDE{b}")
        gone(sq_in.at[b, others], f"SQ{b}")
        gone(x_all.at[b, others], f"X{b}")
        gone(h_in.at[b, others], f"H{b}")
        gone(hid_all.at[b, others], f"HID{b}")
        gone(o_in.at[b, others], f"O{b}")

    def gone_home(core, src, phase):
        own = (c == core) & (xl == c)
        @pl.when(own)
        def _():
            gone(src.at[pl.ds(0, NY - 1)], phase)
        @pl.when(jnp.logical_not(own))
        def _():
            gone(src, phase)

    gone_home(0, stream_out, "STREAM")
    gone_home(1, mix_out, "MIX")
    @pl.when(c == 0)
    def _():
        arrived(out_ref, "STREAM")

    @pl.when(c == 1)
    def _():
        arrived(out_ref, "MIX")


def per_device(
    queries, cache_pool, block_table, cache_len, w_uv, w_out, residual, norm_gain,
    expert_ids, expert_gates, w_gate, w_up, w_down,
):
    hbm = pl.BlockSpec(memory_space=pl.ANY)
    smem = pl.BlockSpec(memory_space=pltpu.SMEM)
    shapes = [
        ((KW, 512), BF16),
        ((64, OWN, KW), BF16),
        ((16, 64, KW), BF16),
        ((LAT, VH), BF16),
        ((1, COLS), F32),
        ((NH, OWN, KW), BF16),
        ((NH, OWN, LAT), BF16),
        ((HB, NZ, 2, OWN, LAT), BF16),
        ((OWN, 128), F32),
        ((NY, OWN, COLS), BF16),
        ((NY, OWN, 128), F32),
        ((NP, VH, COLS), BF16),
        ((NP, COLS, 2 * UNITS), BF16),
        ((NP, UNITS, COLS), BF16),
        ((HB, PART, VH), BF16),
        ((HB, NP, PART, VH), BF16),
        ((HB, NZ, STRIP, COLS), BF16),
        ((HB, NZ, STRIP, COLS), BF16),
        ((NY, OWN, COLS), BF16),
        ((HB, NZ, STRIP, 128), F32),
        ((HB, 8, PART), F32),
        ((HB, NP, 8, PART), F32),
        ((HB, NZ, STRIP, COLS), BF16),
        ((HB, NP, PART, 2 * UNITS), BF16),
        ((HB, NP, PART, 2 * UNITS), BF16),
        ((HB, PART, UNITS), BF16),
        ((HB, NP, PART, UNITS), BF16),
        ((HB, NZ, STRIP, COLS), BF16),
        ((HB, NZ, STRIP, COLS), BF16),
        ((NY, OWN, COLS), BF16),
    ]
    result = pl.pallas_call(
        kernel,
        out_shape=jax.ShapeDtypeStruct((NP, OWN, COLS), BF16),
        in_specs=[hbm, hbm, smem, smem, hbm, hbm, hbm, hbm, smem, smem, hbm, hbm, hbm],
        out_specs=hbm,
        scratch_shapes=[pltpu.VMEM(shape, dtype) for shape, dtype in shapes] + [
            pltpu.SemaphoreType.DMA((4,)),
            pltpu.SemaphoreType.DMA((len(NAMES),)),
            pltpu.SemaphoreType.DMA((len(NAMES),)),
        ],
        compiler_params=pltpu.CompilerParams(
            collective_id=0, has_side_effects=True, vmem_limit_bytes=60 * 1024 * 1024),
        cost_estimate=pl.CostEstimate(
            flops=4_000_000_000, bytes_accessed=16_000_000, transcendentals=400_000),
        name="layer",
    )(
        queries[0, :, 0, :].T, cache_pool[0], block_table[0].T, cache_len,
        w_uv[0], w_out[0], residual[0], norm_gain.reshape(1, D),
        expert_ids[0].T, expert_gates[0].T, w_gate[0], w_up[0], w_down[0],
    )
    return jnp.transpose(result, (1, 0, 2)).reshape(1, 1, OWN, D)


def solution(mesh):
    in_specs = (
        P("sub", None, "head", None),
        P("sub", "head", None, None),
        P("sub", "head", None),
        P("sub", "head"),
        P("head", None, None),
        P("head", None, None),
        P("sub", "head", None),
        P(),
        P("sub", "head", None),
        P("sub", "head", None),
        P("head", None, None),
        P("head", None, None),
        P("head", None, None),
    )
    out_specs = P("side", "sub", "head", None)
    return jax.shard_map(
        per_device, mesh=mesh, in_specs=in_specs, out_specs=out_specs, check_vma=False
    )
```

```python
import jax
import jax.numpy as jnp
from jax import lax
from jax.experimental import pallas as pl
from jax.experimental.pallas import tpu as pltpu
from jax.sharding import PartitionSpec as P

D = 7168
LAT = 512
KW = 576
VH = 128
UNITS = 128
EPS = 1e-6
SCALE = 192 ** (-0.5)

NZ = 8
NP = 8
NY = 4
OWN = 8
COLS = D // NP
CHUNK = NY * OWN
ROWS = NZ * CHUNK
NH = NZ * NY
HB = 2
PART = ROWS // HB
STRIP = CHUNK // HB
MEET = 2 * NH + 2 * NP - 1 + NZ - 1
F32 = jnp.float32
BF16 = jnp.bfloat16


NAMES = (
    ["Q0", "Q1", "RES", "SEL", "LATS", "STREAM", "MIX"]
    + [name + step for name in ("WO", "WG", "WU", "WD") for step in ("", "F")]
    + [name + str(b) for name in ("HEAD", "C", "SIDE", "SQ", "X", "H", "HID", "O") for b in range(HB)]
)
NEAR = 5
SPANS = ((0, NEAR), (NEAR, NZ))
PHASE = {name: i for i, name in enumerate(NAMES)}


def kernel(
    q_ref, pool_ref, tab_ref, len_ref, wuv_ref, wout_ref, res_ref, gain_ref,
    ids_ref, gates_ref, wg_ref, wu_ref, wd_ref,
    out_ref,
    qcols, qrows, pool, wuv, gain, qbuf, lat_out, lat_in, sel, resbuf, selbuf,
    wo, wgu, wd, head_own, head_all, c_out, c_in,
    stream_out, side_all, sq_own, sq_in, x_all,
    h_out, h_in, hid_own, hid_all, o_out, o_in, mix_out,
    tab, lens, ids, gates, load, send, recv,
):
    c = lax.axis_index("side")
    h = lax.axis_index("head")
    sub = lax.axis_index("sub")
    z, n = h // NP, h % NP
    xl, y = n // NY, n % NY
    spot = z * NY + y

    def device(core, head):
        return (core, head, sub)

    def put(src, dst, phase, core, head):
        pltpu.make_async_remote_copy(
            src_ref=src, dst_ref=dst,
            send_sem=send.at[PHASE[phase]], recv_sem=recv.at[PHASE[phase]],
            device_id=device(core, head), device_id_type=pl.DeviceIdType.MESH,
        ).start()

    def keep(src, dst, phase):
        pltpu.make_async_copy(src, dst, recv.at[PHASE[phase]]).start()

    def arrived(ref, phase):
        with jax.named_scope("w_" + phase):
            pltpu.make_async_copy(ref, ref, recv.at[PHASE[phase]]).wait()

    def gone(ref, phase):
        pltpu.make_async_copy(ref, ref, send.at[PHASE[phase]]).wait()

    def loop(count, body):
        def step(k, carry):
            body(k)
            return carry
        lax.fori_loop(0, count, step, 0)

    def around(k, me, size):
        far = (k + 1) // 2
        return (me + size + far * (2 * (k % 2) - 1)) % size

    def depth(k):
        return around(NZ - 1 - k, z, NZ)

    def plane(k):
        turn = jnp.where(k < 2, 2, jnp.where(k < 6, 1 + 2 * (k % 2), 0))
        flip = jnp.where(k < 2, k, jnp.where(k < 4, 0, 1))
        return ((xl + flip) % 2) * NY + (y + turn) % NY

    def cols(m):
        return pl.ds(pl.multiple_of(m * COLS, 128), COLS)

    loads = [
        pltpu.make_async_copy(q_ref, qcols, load.at[0]),
        pltpu.make_async_copy(pool_ref, pool, load.at[1]),
        pltpu.make_async_copy(wuv_ref, wuv, load.at[2]),
        pltpu.make_async_copy(gain_ref.at[:, cols(n)], gain, load.at[3]),
        pltpu.make_async_copy(ids_ref, ids, load.at[4]),
        pltpu.make_async_copy(gates_ref, gates, load.at[5]),
        pltpu.make_async_copy(tab_ref, tab, load.at[6]),
        pltpu.make_async_copy(len_ref, lens, load.at[7]),
    ]
    for copy in loads:
        copy.start()

    barrier = pltpu.get_barrier_semaphore()

    def greet(core, head):
        pl.semaphore_signal(
            barrier, inc=1, device_id=device(core, head), device_id_type=pl.DeviceIdType.MESH)

    def greet_far(level):
        for m in range(NY):
            greet(1 - xl, level * NP + c * NY + m)
            greet(xl, level * NP + (1 - c) * NY + m)
    loop(NZ, greet_far)

    def greet_plane(k):
        m = (c * NP + n + k + 1) % (2 * NP)
        greet(m // NP, z * NP + m % NP)
    loop(2 * NP - 1, greet_plane)

    def greet_depth(k):
        greet(c, depth(k) * NP + n)
    loop(NZ - 1, greet_depth)

    loads[0].wait()
    for i in range(0, KW, 128):
        wide = min(128, KW - i)
        turned = jnp.transpose(qcols[i:i + wide, :].astype(F32))
        qrows[:, :, i:i + wide] = turned.reshape(64, OWN, wide).astype(BF16)

    with jax.named_scope("w_barrier"):
        pl.semaphore_wait(barrier, MEET)

    for a, (first, last) in enumerate(SPANS):
        def send_query(k):
            p = first + k // NY
            level = (z + NZ - around(p, 0, NZ)) % NZ
            owner = level * NP + c * NY + (y + k) % NY
            put(qrows.at[owner], qbuf.at[p * NY + y], f"Q{a}", 1 - xl, owner)
        loop((last - first) * NY, send_query)

    lane = lax.broadcasted_iota(jnp.int32, (OWN, 128), 1)
    line = lax.broadcasted_iota(jnp.int32, (OWN, 128), 0)
    picked = jnp.zeros((OWN, 128), F32)
    loads[4].wait()
    loads[5].wait()
    for r in range(OWN):
        for k in range(ids.shape[0]):
            picked = picked + jnp.where((line == r) & (lane == ids[k, r]), gates[k, r], 0.0)
    sel[...] = picked

    def send_residual(k):
        m = (1 - c) * NY + (y + k) % NY
        put(res_ref.at[:, cols(m)], resbuf.at[y], "RES", xl, z * NP + m)
        put(sel, selbuf.at[y], "SEL", xl, z * NP + m)
    loop(NY, send_residual)

    left, right = pl.ds(0, UNITS), pl.ds(UNITS, UNITS)
    arrays = {
        "WO": (VH, lambda m, i, r: wout_ref.at[r, cols(m)], lambda i, r: wo.at[i, r]),
        "WG": (COLS, lambda m, i, r: wg_ref.at[i], lambda i, r: wgu.at[i, r, left]),
        "WU": (COLS, lambda m, i, r: wu_ref.at[i], lambda i, r: wgu.at[i, r, right]),
        "WD": (UNITS, lambda m, i, r: wd_ref.at[r, cols(m)], lambda i, r: wd.at[i, r]),
    }
    every, others = pl.ds(0, NP), pl.ds(0, NP - 1)

    def halves(name):
        size = arrays[name][0] // 2
        return pl.ds(pl.multiple_of(c * size, size), size)

    def share(name, first=0, last=NP - 1):
        depth_of, source, landing = arrays[name]
        rows = halves(name)
        size = rows.size
        place = landing(n, rows)
        def take(m):
            deep = pl.ds(pl.multiple_of(m * depth_of + rows.start, size), size)
            return source(m, deep, rows)
        if last == NP - 1:
            keep(take(n), place, name)
        def step(k):
            m = plane(k + first)
            put(take(m), place, name, c, z * NP + m)
        loop(last - first, step)

    def pass_on(name):
        mine = arrays[name][2](every, halves(name))
        arrived(mine, name)
        put(mine, mine, name + "F", 1 - c, h)

    def ready(name):
        arrived(arrays[name][2](every, halves(name)), name + "F")

    share("WO")
    row = lax.broadcasted_iota(jnp.int32, (OWN, 1024), 0)
    place = lax.broadcasted_iota(jnp.int32, (OWN, 1024), 1)
    block, offset = place // 64, place % 64
    bias = jnp.full((OWN, 1024), -1e30, F32)
    loads[6].wait()
    loads[7].wait()
    for r in range(OWN):
        seen = ((block == tab[0, r]) & (offset < lens[0, r])) | (
            (block == tab[1, r]) & (offset + 64 < lens[0, r]))
        bias = jnp.where((row == r) & seen, 0.0, bias)


    loads[1].wait()
    keys = pool[...].reshape(1024, KW)
    values = keys[:, :LAT]
    for a, (first, last) in enumerate(SPANS):
        heads_at_once = (last - first) * NY
        some = slice(first * NY, last * NY)
        arrived(qbuf.at[some], f"Q{a}")
        queries = qbuf[some].astype(F32).reshape(heads_at_once * OWN, KW).astype(BF16)
        scores = lax.dot_general(
            queries, keys, (((1,), (1,)), ((), ())), preferred_element_type=F32)
        scores = scores.reshape(heads_at_once, OWN, 1024) * SCALE + bias[None]
        scores = scores.reshape(heads_at_once * OWN, 1024)
        peak = jnp.max(scores, axis=-1, keepdims=True)
        raw = jnp.exp(scores - peak)
        total = jnp.sum(raw, axis=-1, keepdims=True)
        high = raw.astype(BF16)
        low = (raw - high.astype(F32)).astype(BF16)
        latents = jnp.dot(high, values, preferred_element_type=F32)
        latents = (latents + jnp.dot(low, values, preferred_element_type=F32)) / total
        lat_out[some] = latents.reshape(heads_at_once, OWN, LAT).astype(BF16)

        def send_latent(k):
            p, m = first + k // NY, (y + k) % NY
            head = (z + around(p, 0, NZ)) % NZ * NP + (1 - c) * NY + m
            put(lat_out.at[p * NY + m], lat_in.at[y // 2, z, y % 2], "LATS", xl, head)
        loop(heads_at_once, send_latent)

    share("WG", 2)


    loads[2].wait()
    arrived(lat_in, "LATS")
    for b in range(HB):
        rows = lat_in[b].astype(F32).reshape(PART, LAT).astype(BF16)
        head_own[b] = jnp.dot(rows, wuv[...], preferred_element_type=F32).astype(BF16)
        keep(head_own.at[b], head_all.at[b, n], f"HEAD{b}")
        def send_head(k):
            put(head_own.at[b], head_all.at[b, n], f"HEAD{b}", c, z * NP + plane(k))
        loop(NP - 1, send_head)

    pass_on("WO")
    share("WG", 0, 2)
    share("WU")
    ready("WO")
    for b in range(HB):
        arrived(head_all.at[b], f"HEAD{b}")
        heads = jnp.concatenate([head_all[b, i] for i in range(NP)], axis=1)
        partial = jnp.dot(heads, wo[...].reshape(NP * VH, COLS), preferred_element_type=F32)
        c_out[b] = partial.astype(BF16).reshape(NZ, STRIP, COLS)
        keep(c_out.at[b, z], c_in.at[b, z], f"C{b}")
        def send_c(k):
            m = depth(k)
            put(c_out.at[b, m], c_in.at[b, z], f"C{b}", c, m * NP + n)
        loop(NZ - 1, send_c)

    share("WD")

    def home(core, src, landing, phase, k):
        own = (c == core) & (xl == c) & (y == k)
        @pl.when(own)
        def _():
            keep(src.at[k], landing.at[n], phase)
        @pl.when(jnp.logical_not(own))
        def _():
            put(src.at[k], landing.at[n], phase, core, z * NP + c * NY + k)

    arrived(resbuf, "RES")
    arrived(selbuf, "SEL")
    loads[3].wait()
    for b in range(HB):
        pair = slice(2 * b, 2 * b + 2)
        arrived(c_in.at[b], f"C{b}")
        attended = c_in[b, 0].astype(F32)
        for i in range(1, NZ):
            attended = attended + c_in[b, i].astype(F32)
        residual = resbuf[pair].astype(F32).reshape(STRIP, COLS)
        stream = (residual + attended).astype(BF16).astype(F32)
        x_all[b, z] = (stream * gain[...]).astype(BF16)
        def send_x(k):
            put(x_all.at[b, z], x_all.at[b, z], f"X{b}", c, depth(k) * NP + n)
        loop(NZ - 1, send_x)

        squares = jnp.sum(stream * stream, axis=-1, keepdims=True)
        wide = lax.broadcasted_iota(jnp.int32, (STRIP, 128), 1)
        chosen = selbuf[pair].reshape(STRIP, 128)
        side_all[b, z] = jnp.where(wide < 8, chosen, squares)
        def send_side(k):
            put(side_all.at[b, z], side_all.at[b, z], f"SIDE{b}", c, depth(k) * NP + n)
        loop(NZ - 1, send_side)

        stream_out[pair] = stream.reshape(2, OWN, COLS).astype(BF16)

    pass_on("WG")
    pass_on("WU")

    ready("WG")
    ready("WU")
    lanes = lax.broadcasted_iota(jnp.int32, (PART, 128), 1)
    gate_of = []

    def begin(b):
        arrived(side_all.at[b, others], f"SIDE{b}")
        tiles = side_all[b].reshape(PART, 128)
        gate_of.append(jnp.sum(jnp.where(lanes == z, tiles, 0.0), axis=-1, keepdims=True))
        sq_own[b] = jnp.transpose(tiles)[8:16]
        keep(sq_own.at[b], sq_in.at[b, n], f"SQ{b}")
        def send_sq(k):
            put(sq_own.at[b], sq_in.at[b, n], f"SQ{b}", c, z * NP + plane(k))
        loop(NP - 1, send_sq)

    def lift(b, first, last):
        arrived(x_all.at[b, others], f"X{b}")
        x = x_all[b].reshape(PART, COLS)
        def send_h(k):
            m = plane(k + first)
            h_out[b, m] = jnp.dot(x, wgu[m], preferred_element_type=F32).astype(BF16)
            put(h_out.at[b, m], h_in.at[b, n], f"H{b}", c, z * NP + m)
        loop(last - first, send_h)
        if last == NP - 1:
            h_out[b, n] = jnp.dot(x, wgu[n], preferred_element_type=F32).astype(BF16)
            keep(h_out.at[b, n], h_in.at[b, n], f"H{b}")

    def join(b):
        arrived(sq_in.at[b], f"SQ{b}")
        square = sq_in[b, 0]
        for i in range(1, NP):
            square = square + sq_in[b, i]
        scale = lax.rsqrt(square * (1.0 / D) + EPS)
        scale = jnp.transpose(jnp.broadcast_to(scale[0:1], (128, PART)))

        arrived(h_in.at[b], f"H{b}")
        products = h_in[b, 0].astype(F32)
        for i in range(1, NP):
            products = products + h_in[b, i].astype(F32)
        gated = products[:, :UNITS] * scale
        lifted = products[:, UNITS:] * scale
        hid_own[b] = (gated * jax.nn.sigmoid(gated) * lifted).astype(BF16)
        keep(hid_own.at[b], hid_all.at[b, n], f"HID{b}")
        def send_hid(k):
            put(hid_own.at[b], hid_all.at[b, n], f"HID{b}", c, z * NP + plane(k))
        loop(NP - 1, send_hid)

    lift(0, 0, NP - 1)
    begin(0)
    lift(1, 0, NP - 1)
    begin(1)
    pass_on("WD")
    join(0)
    join(1)

    ready("WD")
    for b in range(HB):
        arrived(hid_all.at[b], f"HID{b}")
        hidden = jnp.concatenate([hid_all[b, i] for i in range(NP)], axis=1)
        expert = jnp.dot(hidden, wd[...].reshape(NP * UNITS, COLS), preferred_element_type=F32)
        o_out[b] = (expert * gate_of[b]).astype(BF16).reshape(NZ, STRIP, COLS)
        keep(o_out.at[b, z], o_in.at[b, z], f"O{b}")
        def send_o(k):
            m = depth(k)
            put(o_out.at[b, m], o_in.at[b, z], f"O{b}", c, m * NP + n)
        loop(NZ - 1, send_o)

    for k in range(NY):
        home(0, stream_out, out_ref, "STREAM", k)

    for b in range(HB):
        arrived(o_in.at[b], f"O{b}")
        mixture = o_in[b, 0].astype(F32)
        for i in range(1, NZ):
            mixture = mixture + o_in[b, i].astype(F32)
        mix_out[2 * b:2 * b + 2] = mixture.reshape(2, OWN, COLS).astype(BF16)
        home(1, mix_out, out_ref, "MIX", 2 * b)
        home(1, mix_out, out_ref, "MIX", 2 * b + 1)

    for a, (first, last) in enumerate(SPANS):
        gone(qbuf.at[first * NY:last * NY], f"Q{a}")
    gone(resbuf, "RES")
    gone(selbuf, "SEL")
    gone(lat_in, "LATS")
    for name, (_, _, landing) in arrays.items():
        gone(landing(others, halves(name)), name)
        gone(landing(every, halves(name)), name + "F")
    for b in range(HB):
        gone(head_all.at[b, others], f"HEAD{b}")
        gone(c_in.at[b, others], f"C{b}")
        gone(side_all.at[b, others], f"SIDE{b}")
        gone(sq_in.at[b, others], f"SQ{b}")
        gone(x_all.at[b, others], f"X{b}")
        gone(h_in.at[b, others], f"H{b}")
        gone(hid_all.at[b, others], f"HID{b}")
        gone(o_in.at[b, others], f"O{b}")

    def gone_home(core, src, phase):
        own = (c == core) & (xl == c)
        @pl.when(own)
        def _():
            gone(src.at[pl.ds(0, NY - 1)], phase)
        @pl.when(jnp.logical_not(own))
        def _():
            gone(src, phase)

    gone_home(0, stream_out, "STREAM")
    gone_home(1, mix_out, "MIX")
    @pl.when(c == 0)
    def _():
        arrived(out_ref, "STREAM")

    @pl.when(c == 1)
    def _():
        arrived(out_ref, "MIX")


def per_device(
    queries, cache_pool, block_table, cache_len, w_uv, w_out, residual, norm_gain,
    expert_ids, expert_gates, w_gate, w_up, w_down,
):
    hbm = pl.BlockSpec(memory_space=pl.ANY)
    shapes = [
        ((KW, 512), BF16),
        ((64, OWN, KW), BF16),
        ((16, 64, KW), BF16),
        ((LAT, VH), BF16),
        ((1, COLS), F32),
        ((NH, OWN, KW), BF16),
        ((NH, OWN, LAT), BF16),
        ((HB, NZ, 2, OWN, LAT), BF16),
        ((OWN, 128), F32),
        ((NY, OWN, COLS), BF16),
        ((NY, OWN, 128), F32),
        ((NP, VH, COLS), BF16),
        ((NP, COLS, 2 * UNITS), BF16),
        ((NP, UNITS, COLS), BF16),
        ((HB, PART, VH), BF16),
        ((HB, NP, PART, VH), BF16),
        ((HB, NZ, STRIP, COLS), BF16),
        ((HB, NZ, STRIP, COLS), BF16),
        ((NY, OWN, COLS), BF16),
        ((HB, NZ, STRIP, 128), F32),
        ((HB, 8, PART), F32),
        ((HB, NP, 8, PART), F32),
        ((HB, NZ, STRIP, COLS), BF16),
        ((HB, NP, PART, 2 * UNITS), BF16),
        ((HB, NP, PART, 2 * UNITS), BF16),
        ((HB, PART, UNITS), BF16),
        ((HB, NP, PART, UNITS), BF16),
        ((HB, NZ, STRIP, COLS), BF16),
        ((HB, NZ, STRIP, COLS), BF16),
        ((NY, OWN, COLS), BF16),
    ]
    result = pl.pallas_call(
        kernel,
        out_shape=jax.ShapeDtypeStruct((NP, OWN, COLS), BF16),
        in_specs=[hbm] * 13,
        out_specs=hbm,
        scratch_shapes=[pltpu.VMEM(shape, dtype) for shape, dtype in shapes] + [
            pltpu.SMEM((2, OWN), jnp.int32),
            pltpu.SMEM((1, OWN), jnp.int32),
            pltpu.SMEM((4, OWN), jnp.int32),
            pltpu.SMEM((4, OWN), F32),
            pltpu.SemaphoreType.DMA((8,)),
            pltpu.SemaphoreType.DMA((len(NAMES),)),
            pltpu.SemaphoreType.DMA((len(NAMES),)),
        ],
        compiler_params=pltpu.CompilerParams(
            collective_id=0, has_side_effects=True, vmem_limit_bytes=60 * 1024 * 1024),
        cost_estimate=pl.CostEstimate(
            flops=4_000_000_000, bytes_accessed=16_000_000, transcendentals=400_000),
        name="layer",
    )(
        queries[0, :, 0, :].T, cache_pool[0], block_table[0].T, cache_len,
        w_uv[0], w_out[0], residual[0], norm_gain.reshape(1, D),
        expert_ids[0].T, expert_gates[0].T, w_gate[0], w_up[0], w_down[0],
    )
    return jnp.transpose(result, (1, 0, 2)).reshape(1, 1, OWN, D)


def solution(mesh):
    in_specs = (
        P("sub", None, "head", None),
        P("sub", "head", None, None),
        P("sub", "head", None),
        P("sub", "head"),
        P("head", None, None),
        P("head", None, None),
        P("sub", "head", None),
        P(),
        P("sub", "head", None),
        P("sub", "head", None),
        P("head", None, None),
        P("head", None, None),
        P("head", None, None),
    )
    out_specs = P("side", "sub", "head", None)
    return jax.shard_map(
        per_device, mesh=mesh, in_specs=in_specs, out_specs=out_specs, check_vma=False
    )
```

```python
import jax
import jax.numpy as jnp
from jax import lax
from jax.experimental import pallas as pl
from jax.experimental.pallas import tpu as pltpu
from jax.sharding import PartitionSpec as P

D = 7168
LAT = 512
KW = 576
VH = 128
UNITS = 128
EPS = 1e-6
SCALE = 192 ** (-0.5)

NZ = 8
NP = 8
NY = 4
OWN = 8
COLS = D // NP
CHUNK = NY * OWN
ROWS = NZ * CHUNK
NH = NZ * NY
HB = 2
PART = ROWS // HB
STRIP = CHUNK // HB
MEET = 2 * NH + 2 * NP - 1 + NZ - 1
F32 = jnp.float32
BF16 = jnp.bfloat16


NAMES = (
    ["Q0", "Q1", "RES", "SEL", "LATS", "STREAM", "MIX"]
    + [name + step for name in ("WO", "WG", "WU", "WD") for step in ("", "F")]
    + [name + str(b) for name in ("HEAD", "C", "SIDE", "SQ", "X", "H", "HID", "O") for b in range(HB)]
)
NEAR = 5
SPANS = ((0, NEAR), (NEAR, NZ))
PHASE = {name: i for i, name in enumerate(NAMES)}


def kernel(
    q_ref, pool_ref, tab_ref, len_ref, wuv_ref, wout_ref, res_ref, gain_ref,
    ids_ref, gates_ref, wg_ref, wu_ref, wd_ref,
    out_ref,
    qcols, qrows, pool, wuv, gain, qbuf, lat_out, lat_in, sel, resbuf, selbuf,
    wo, wgu, wd, head_own, head_all, c_out, c_in,
    stream_out, side_all, sq_own, sq_in, x_all,
    h_out, h_in, hid_own, hid_all, o_out, o_in, mix_out,
    tab, lens, ids, gates, load, send, recv,
):
    c = lax.axis_index("side")
    h = lax.axis_index("head")
    sub = lax.axis_index("sub")
    z, n = h // NP, h % NP
    xl, y = n // NY, n % NY
    spot = z * NY + y

    def device(core, head):
        return (core, head, sub)

    def put(src, dst, phase, core, head):
        pltpu.make_async_remote_copy(
            src_ref=src, dst_ref=dst,
            send_sem=send.at[PHASE[phase]], recv_sem=recv.at[PHASE[phase]],
            device_id=device(core, head), device_id_type=pl.DeviceIdType.MESH,
        ).start()

    def keep(src, dst, phase):
        pltpu.make_async_copy(src, dst, recv.at[PHASE[phase]]).start()

    def arrived(ref, phase):
        with jax.named_scope("w_" + phase):
            pltpu.make_async_copy(ref, ref, recv.at[PHASE[phase]]).wait()

    def gone(ref, phase):
        pltpu.make_async_copy(ref, ref, send.at[PHASE[phase]]).wait()

    def loop(count, body):
        def step(k, carry):
            body(k)
            return carry
        lax.fori_loop(0, count, step, 0)

    def around(k, me, size):
        far = (k + 1) // 2
        return (me + size + far * (2 * (k % 2) - 1)) % size

    def depth(k):
        return around(NZ - 1 - k, z, NZ)

    def plane(k):
        turn = jnp.where(k < 2, 2, jnp.where(k < 6, 1 + 2 * (k % 2), 0))
        flip = jnp.where(k < 2, k, jnp.where(k < 4, 0, 1))
        return ((xl + flip) % 2) * NY + (y + turn) % NY

    def cols(m):
        return pl.ds(pl.multiple_of(m * COLS, 128), COLS)

    loads = [
        pltpu.make_async_copy(q_ref, qcols, load.at[0]),
        pltpu.make_async_copy(pool_ref, pool, load.at[1]),
        pltpu.make_async_copy(wuv_ref, wuv, load.at[2]),
        pltpu.make_async_copy(gain_ref.at[:, cols(n)], gain, load.at[3]),
        pltpu.make_async_copy(ids_ref, ids, load.at[4]),
        pltpu.make_async_copy(gates_ref, gates, load.at[5]),
        pltpu.make_async_copy(tab_ref, tab, load.at[6]),
        pltpu.make_async_copy(len_ref, lens, load.at[7]),
    ]
    for copy in loads:
        copy.start()

    barrier = pltpu.get_barrier_semaphore()

    def greet(core, head):
        pl.semaphore_signal(
            barrier, inc=1, device_id=device(core, head), device_id_type=pl.DeviceIdType.MESH)

    def greet_far(level):
        for m in range(NY):
            greet(1 - xl, level * NP + c * NY + m)
            greet(xl, level * NP + (1 - c) * NY + m)
    loop(NZ, greet_far)

    def greet_plane(k):
        m = (c * NP + n + k + 1) % (2 * NP)
        greet(m // NP, z * NP + m % NP)
    for k in range(2 * NP - 1):
        greet_plane(k)

    for k in range(1, NZ):
        greet(c, (z + k) % NZ * NP + n)

    loads[0].wait()
    for i in range(0, KW, 128):
        wide = min(128, KW - i)
        turned = jnp.transpose(qcols[i:i + wide, :].astype(F32))
        qrows[:, :, i:i + wide] = turned.reshape(64, OWN, wide).astype(BF16)

    with jax.named_scope("w_barrier"):
        pl.semaphore_wait(barrier, MEET)

    for a, (first, last) in enumerate(SPANS):
        def send_query(k):
            p = first + k // NY
            level = (z + NZ - around(p, 0, NZ)) % NZ
            owner = level * NP + c * NY + (y + k) % NY
            put(qrows.at[owner], qbuf.at[p * NY + y], f"Q{a}", 1 - xl, owner)
        loop((last - first) * NY, send_query)

    lane = lax.broadcasted_iota(jnp.int32, (OWN, 128), 1)
    line = lax.broadcasted_iota(jnp.int32, (OWN, 128), 0)
    picked = jnp.zeros((OWN, 128), F32)
    loads[4].wait()
    loads[5].wait()
    for r in range(OWN):
        for k in range(ids.shape[0]):
            picked = picked + jnp.where((line == r) & (lane == ids[k, r]), gates[k, r], 0.0)
    sel[...] = picked

    def send_residual(k):
        m = (1 - c) * NY + (y + k) % NY
        put(res_ref.at[:, cols(m)], resbuf.at[y], "RES", xl, z * NP + m)
        put(sel, selbuf.at[y], "SEL", xl, z * NP + m)
    loop(NY, send_residual)

    left, right = pl.ds(0, UNITS), pl.ds(UNITS, UNITS)
    arrays = {
        "WO": (VH, lambda m, i, r: wout_ref.at[r, cols(m)], lambda i, r: wo.at[i, r]),
        "WG": (COLS, lambda m, i, r: wg_ref.at[i], lambda i, r: wgu.at[i, r, left]),
        "WU": (COLS, lambda m, i, r: wu_ref.at[i], lambda i, r: wgu.at[i, r, right]),
        "WD": (UNITS, lambda m, i, r: wd_ref.at[r, cols(m)], lambda i, r: wd.at[i, r]),
    }
    every, others = pl.ds(0, NP), pl.ds(0, NP - 1)

    def halves(name):
        size = arrays[name][0] // 2
        return pl.ds(pl.multiple_of(c * size, size), size)

    def share(name, first=0, last=NP - 1):
        depth_of, source, landing = arrays[name]
        rows = halves(name)
        size = rows.size
        place = landing(n, rows)
        def take(m):
            deep = pl.ds(pl.multiple_of(m * depth_of + rows.start, size), size)
            return source(m, deep, rows)
        if last == NP - 1:
            keep(take(n), place, name)
        def step(k):
            m = plane(k + first)
            put(take(m), place, name, c, z * NP + m)
        loop(last - first, step)

    def pass_on(name):
        mine = arrays[name][2](every, halves(name))
        arrived(mine, name)
        put(mine, mine, name + "F", 1 - c, h)

    def ready(name):
        arrived(arrays[name][2](every, halves(name)), name + "F")

    share("WO")
    row = lax.broadcasted_iota(jnp.int32, (OWN, 1024), 0)
    place = lax.broadcasted_iota(jnp.int32, (OWN, 1024), 1)
    block, offset = place // 64, place % 64
    bias = jnp.full((OWN, 1024), -1e30, F32)
    loads[6].wait()
    loads[7].wait()
    for r in range(OWN):
        seen = ((block == tab[0, r]) & (offset < lens[0, r])) | (
            (block == tab[1, r]) & (offset + 64 < lens[0, r]))
        bias = jnp.where((row == r) & seen, 0.0, bias)


    loads[1].wait()
    keys = pool[...].reshape(1024, KW)
    values = keys[:, :LAT]
    for a, (first, last) in enumerate(SPANS):
        heads_at_once = (last - first) * NY
        some = slice(first * NY, last * NY)
        arrived(qbuf.at[some], f"Q{a}")
        queries = qbuf[some].astype(F32).reshape(heads_at_once * OWN, KW).astype(BF16)
        scores = lax.dot_general(
            queries, keys, (((1,), (1,)), ((), ())), preferred_element_type=F32)
        scores = scores.reshape(heads_at_once, OWN, 1024) * SCALE + bias[None]
        scores = scores.reshape(heads_at_once * OWN, 1024)
        peak = jnp.max(scores, axis=-1, keepdims=True)
        raw = jnp.exp(scores - peak)
        total = jnp.sum(raw, axis=-1, keepdims=True)
        high = raw.astype(BF16)
        low = (raw - high.astype(F32)).astype(BF16)
        latents = jnp.dot(high, values, preferred_element_type=F32)
        latents = (latents + jnp.dot(low, values, preferred_element_type=F32)) / total
        lat_out[some] = latents.reshape(heads_at_once, OWN, LAT).astype(BF16)

        def send_latent(k):
            p, m = first + k // NY, (y + k) % NY
            head = (z + around(p, 0, NZ)) % NZ * NP + (1 - c) * NY + m
            put(lat_out.at[p * NY + m], lat_in.at[y // 2, z, y % 2], "LATS", xl, head)
        loop(heads_at_once, send_latent)

    share("WG", 2)


    loads[2].wait()
    arrived(lat_in, "LATS")
    for b in range(HB):
        rows = lat_in[b].astype(F32).reshape(PART, LAT).astype(BF16)
        head_own[b] = jnp.dot(rows, wuv[...], preferred_element_type=F32).astype(BF16)
        keep(head_own.at[b], head_all.at[b, n], f"HEAD{b}")
        def send_head(k):
            put(head_own.at[b], head_all.at[b, n], f"HEAD{b}", c, z * NP + plane(k))
        loop(NP - 1, send_head)

    pass_on("WO")
    share("WG", 0, 2)
    share("WU")
    ready("WO")
    for b in range(HB):
        arrived(head_all.at[b], f"HEAD{b}")
        heads = jnp.concatenate([head_all[b, i] for i in range(NP)], axis=1)
        partial = jnp.dot(heads, wo[...].reshape(NP * VH, COLS), preferred_element_type=F32)
        c_out[b] = partial.astype(BF16).reshape(NZ, STRIP, COLS)
        keep(c_out.at[b, z], c_in.at[b, z], f"C{b}")
        def send_c(k):
            m = depth(k)
            put(c_out.at[b, m], c_in.at[b, z], f"C{b}", c, m * NP + n)
        loop(NZ - 1, send_c)

    share("WD")

    def home(core, src, landing, phase, k):
        own = (c == core) & (xl == c) & (y == k)
        @pl.when(own)
        def _():
            keep(src.at[k], landing.at[n], phase)
        @pl.when(jnp.logical_not(own))
        def _():
            put(src.at[k], landing.at[n], phase, core, z * NP + c * NY + k)

    arrived(resbuf, "RES")
    arrived(selbuf, "SEL")
    loads[3].wait()
    for b in range(HB):
        pair = slice(2 * b, 2 * b + 2)
        arrived(c_in.at[b], f"C{b}")
        attended = c_in[b, 0].astype(F32)
        for i in range(1, NZ):
            attended = attended + c_in[b, i].astype(F32)
        residual = resbuf[pair].astype(F32).reshape(STRIP, COLS)
        stream = (residual + attended).astype(BF16).astype(F32)
        x_all[b, z] = (stream * gain[...]).astype(BF16)
        def send_x(k):
            put(x_all.at[b, z], x_all.at[b, z], f"X{b}", c, depth(k) * NP + n)
        loop(NZ - 1, send_x)

        squares = jnp.sum(stream * stream, axis=-1, keepdims=True)
        wide = lax.broadcasted_iota(jnp.int32, (STRIP, 128), 1)
        chosen = selbuf[pair].reshape(STRIP, 128)
        side_all[b, z] = jnp.where(wide < 8, chosen, squares)
        def send_side(k):
            put(side_all.at[b, z], side_all.at[b, z], f"SIDE{b}", c, depth(k) * NP + n)
        loop(NZ - 1, send_side)

        stream_out[pair] = stream.reshape(2, OWN, COLS).astype(BF16)

    pass_on("WG")
    pass_on("WU")

    ready("WG")
    ready("WU")
    lanes = lax.broadcasted_iota(jnp.int32, (PART, 128), 1)
    gate_of = []

    def begin(b):
        arrived(side_all.at[b, others], f"SIDE{b}")
        tiles = side_all[b].reshape(PART, 128)
        gate_of.append(jnp.sum(jnp.where(lanes == z, tiles, 0.0), axis=-1, keepdims=True))
        sq_own[b] = jnp.transpose(tiles)[8:16]
        keep(sq_own.at[b], sq_in.at[b, n], f"SQ{b}")
        def send_sq(k):
            put(sq_own.at[b], sq_in.at[b, n], f"SQ{b}", c, z * NP + plane(k))
        loop(NP - 1, send_sq)

    def lift(b, first, last):
        arrived(x_all.at[b, others], f"X{b}")
        x = x_all[b].reshape(PART, COLS)
        def send_h(k):
            m = plane(k + first)
            h_out[b, m] = jnp.dot(x, wgu[m], preferred_element_type=F32).astype(BF16)
            put(h_out.at[b, m], h_in.at[b, n], f"H{b}", c, z * NP + m)
        loop(last - first, send_h)
        if last == NP - 1:
            h_out[b, n] = jnp.dot(x, wgu[n], preferred_element_type=F32).astype(BF16)
            keep(h_out.at[b, n], h_in.at[b, n], f"H{b}")

    def join(b):
        arrived(sq_in.at[b], f"SQ{b}")
        square = sq_in[b, 0]
        for i in range(1, NP):
            square = square + sq_in[b, i]
        scale = lax.rsqrt(square * (1.0 / D) + EPS)
        scale = jnp.transpose(jnp.broadcast_to(scale[0:1], (128, PART)))

        arrived(h_in.at[b], f"H{b}")
        products = h_in[b, 0].astype(F32)
        for i in range(1, NP):
            products = products + h_in[b, i].astype(F32)
        gated = products[:, :UNITS] * scale
        lifted = products[:, UNITS:] * scale
        hid_own[b] = (gated * jax.nn.sigmoid(gated) * lifted).astype(BF16)
        keep(hid_own.at[b], hid_all.at[b, n], f"HID{b}")
        def send_hid(k):
            put(hid_own.at[b], hid_all.at[b, n], f"HID{b}", c, z * NP + plane(k))
        loop(NP - 1, send_hid)

    lift(0, 0, NP - 1)
    begin(0)
    lift(1, 0, NP - 1)
    begin(1)
    pass_on("WD")
    join(0)
    join(1)

    ready("WD")
    for b in range(HB):
        arrived(hid_all.at[b], f"HID{b}")
        hidden = jnp.concatenate([hid_all[b, i] for i in range(NP)], axis=1)
        expert = jnp.dot(hidden, wd[...].reshape(NP * UNITS, COLS), preferred_element_type=F32)
        o_out[b] = (expert * gate_of[b]).astype(BF16).reshape(NZ, STRIP, COLS)
        keep(o_out.at[b, z], o_in.at[b, z], f"O{b}")
        def send_o(k):
            m = depth(k)
            put(o_out.at[b, m], o_in.at[b, z], f"O{b}", c, m * NP + n)
        loop(NZ - 1, send_o)

    for k in range(NY):
        home(0, stream_out, out_ref, "STREAM", k)

    for b in range(HB):
        arrived(o_in.at[b], f"O{b}")
        mixture = o_in[b, 0].astype(F32)
        for i in range(1, NZ):
            mixture = mixture + o_in[b, i].astype(F32)
        mix_out[2 * b:2 * b + 2] = mixture.reshape(2, OWN, COLS).astype(BF16)
        home(1, mix_out, out_ref, "MIX", 2 * b)
        home(1, mix_out, out_ref, "MIX", 2 * b + 1)

    for a, (first, last) in enumerate(SPANS):
        gone(qbuf.at[first * NY:last * NY], f"Q{a}")
    gone(resbuf, "RES")
    gone(selbuf, "SEL")
    gone(lat_in, "LATS")
    for name, (_, _, landing) in arrays.items():
        gone(landing(others, halves(name)), name)
        gone(landing(every, halves(name)), name + "F")
    for b in range(HB):
        gone(head_all.at[b, others], f"HEAD{b}")
        gone(c_in.at[b, others], f"C{b}")
        gone(side_all.at[b, others], f"SIDE{b}")
        gone(sq_in.at[b, others], f"SQ{b}")
        gone(x_all.at[b, others], f"X{b}")
        gone(h_in.at[b, others], f"H{b}")
        gone(hid_all.at[b, others], f"HID{b}")
        gone(o_in.at[b, others], f"O{b}")

    def gone_home(core, src, phase):
        own = (c == core) & (xl == c)
        @pl.when(own)
        def _():
            gone(src.at[pl.ds(0, NY - 1)], phase)
        @pl.when(jnp.logical_not(own))
        def _():
            gone(src, phase)

    gone_home(0, stream_out, "STREAM")
    gone_home(1, mix_out, "MIX")
    @pl.when(c == 0)
    def _():
        arrived(out_ref, "STREAM")

    @pl.when(c == 1)
    def _():
        arrived(out_ref, "MIX")


def per_device(
    queries, cache_pool, block_table, cache_len, w_uv, w_out, residual, norm_gain,
    expert_ids, expert_gates, w_gate, w_up, w_down,
):
    hbm = pl.BlockSpec(memory_space=pl.ANY)
    shapes = [
        ((KW, 512), BF16),
        ((64, OWN, KW), BF16),
        ((16, 64, KW), BF16),
        ((LAT, VH), BF16),
        ((1, COLS), F32),
        ((NH, OWN, KW), BF16),
        ((NH, OWN, LAT), BF16),
        ((HB, NZ, 2, OWN, LAT), BF16),
        ((OWN, 128), F32),
        ((NY, OWN, COLS), BF16),
        ((NY, OWN, 128), F32),
        ((NP, VH, COLS), BF16),
        ((NP, COLS, 2 * UNITS), BF16),
        ((NP, UNITS, COLS), BF16),
        ((HB, PART, VH), BF16),
        ((HB, NP, PART, VH), BF16),
        ((HB, NZ, STRIP, COLS), BF16),
        ((HB, NZ, STRIP, COLS), BF16),
        ((NY, OWN, COLS), BF16),
        ((HB, NZ, STRIP, 128), F32),
        ((HB, 8, PART), F32),
        ((HB, NP, 8, PART), F32),
        ((HB, NZ, STRIP, COLS), BF16),
        ((HB, NP, PART, 2 * UNITS), BF16),
        ((HB, NP, PART, 2 * UNITS), BF16),
        ((HB, PART, UNITS), BF16),
        ((HB, NP, PART, UNITS), BF16),
        ((HB, NZ, STRIP, COLS), BF16),
        ((HB, NZ, STRIP, COLS), BF16),
        ((NY, OWN, COLS), BF16),
    ]
    result = pl.pallas_call(
        kernel,
        out_shape=jax.ShapeDtypeStruct((NP, OWN, COLS), BF16),
        in_specs=[hbm] * 13,
        out_specs=hbm,
        scratch_shapes=[pltpu.VMEM(shape, dtype) for shape, dtype in shapes] + [
            pltpu.SMEM((2, OWN), jnp.int32),
            pltpu.SMEM((1, OWN), jnp.int32),
            pltpu.SMEM((4, OWN), jnp.int32),
            pltpu.SMEM((4, OWN), F32),
            pltpu.SemaphoreType.DMA((8,)),
            pltpu.SemaphoreType.DMA((len(NAMES),)),
            pltpu.SemaphoreType.DMA((len(NAMES),)),
        ],
        compiler_params=pltpu.CompilerParams(
            collective_id=0, has_side_effects=True, vmem_limit_bytes=60 * 1024 * 1024),
        cost_estimate=pl.CostEstimate(
            flops=4_000_000_000, bytes_accessed=16_000_000, transcendentals=400_000),
        name="layer",
    )(
        queries[0, :, 0, :].T, cache_pool[0], block_table[0].T, cache_len,
        w_uv[0], w_out[0], residual[0], norm_gain.reshape(1, D),
        expert_ids[0].T, expert_gates[0].T, w_gate[0], w_up[0], w_down[0],
    )
    return jnp.transpose(result, (1, 0, 2)).reshape(1, 1, OWN, D)


def solution(mesh):
    in_specs = (
        P("sub", None, "head", None),
        P("sub", "head", None, None),
        P("sub", "head", None),
        P("sub", "head"),
        P("head", None, None),
        P("head", None, None),
        P("sub", "head", None),
        P(),
        P("sub", "head", None),
        P("sub", "head", None),
        P("head", None, None),
        P("head", None, None),
        P("head", None, None),
    )
    out_specs = P("side", "sub", "head", None)
    return jax.shard_map(
        per_device, mesh=mesh, in_specs=in_specs, out_specs=out_specs, check_vma=False
    )
```
